128 devices in a mesh: row: 8 (over y, core), col: 16 (over x, z).
Axes of the slice: x: 4, y: 4, z: 4, core: 2. Of those that a mesh axis runs over, the one named last changes fastest.
Arguments:
- features: bfloat16 [65536, 128], P(('col', 'row')), may hold values from -6 to 6
- weight: bfloat16 [128, 128], replicated, may hold values from -0.5 to 0.5
- adjacency: bfloat16 [8, 16, 512, 128, 128], P('row', 'col'), may hold values from -0.046875 to 0.046875
- row_index: int32 [8, 16, 512], P('row', 'col'), may hold values from 0 to 63
- col_index: int32 [8, 16, 512], P('row', 'col'), may hold values from 0 to 31
- block_count: int32 [8, 16], P('row', 'col'), may hold values from 170 to 512, as said below
- grad_out: bfloat16 [65536, 128], P(('row', 'col')), may hold values from -6 to 6
Outputs:
- activated: bfloat16 [65536, 128], P(('row', 'col'))
- input_grad: bfloat16 [65536, 128], P(('col', 'row'))
- weight_grad: float32 [128, 128], replicated
The draws below stay inside these ranges and needn't reach their ends.
Inputs may be any that keep to these rules, and one draw needn't show every extreme that they name: `block_count`: slots at or beyond a position's count hold arbitrary values and indices and are ignored; some position holds exactly 512 live slots in every draw. `row_index`: several slots may name the same block; their values add.
All inputs are finite; a program needn't handle non-finite values.
Results may differ from the reference program's by a relative error of at most 0.0075.
Values may be sent and summed in bfloat16 or wider, within the bound.
No kernel may reach another device: no remote copies, remote signals or barrier semaphores. Data moves between devices by JAX's collectives and lax.ppermute only.
A program may use at most 192 MiB of HBM per device.

```python
import jax
import jax.numpy as jnp
from jax import lax

F = 128
BLK = 128
NB_DEV = 4
BLK_DEV = 512
NODES = 65536
RB = 64
CB = 32
N_ROW = 8
N_COL = 16


def draw_block_count(key, part):
    key = jax.random.fold_in(key, 7)
    first, second = jax.random.split(key)
    counts = jax.random.randint(first, (N_ROW * N_COL,), max(1, BLK_DEV // 3), BLK_DEV + 1)
    fullest = jax.random.randint(second, (), 0, N_ROW * N_COL)
    counts = counts.at[fullest].set(BLK_DEV)
    return counts.reshape(N_ROW, N_COL).astype(jnp.int32)


def place_ends(values, key, smallest, top_value):
    longest = values.shape.index(max(values.shape))
    spots = []
    for shift in (0, 1):
        where = [jax.random.randint(jax.random.fold_in(key, axis), (), 0, length) for axis, length in enumerate(values.shape)]
        where[longest] = (where[longest] + shift) % values.shape[longest]
        spots.append(tuple(where))
    return values.at[spots[0]].set(smallest).at[spots[1]].set(top_value)


def steps_of(key, shape, cuts, least, high):
    loudness = 1.0
    for position, shards_of in cuts:
        steps = jax.random.uniform(jax.random.fold_in(jax.random.fold_in(key, 6), position), (shards_of,), jnp.float32, least / len(cuts), high / len(cuts))
        loudness = loudness * jnp.repeat(jnp.exp(steps), shape[position] // shards_of).reshape((-1,) + (1,) * (len(shape) - 1 - position))
    return loudness


def scatter_about(rng, extent, scale, limit, cuts=(), held_as=jnp.bfloat16):
    gain = steps_of(rng, extent, cuts, -0.22, 0.18) if cuts else 1.0
    result = jax.random.normal(rng, extent, jnp.float32) * scale * gain
    return jnp.minimum(jnp.maximum(result, -limit), limit).astype(held_as)


def setup_inputs(seed: int = 0) -> dict:
    key_of = jax.random.split(jax.random.key(seed), 8)
    features = scatter_about(key_of[0], (NODES, F), 1.0, 6.0, ((0, 128),))
    weight = scatter_about(key_of[1], (F, F), F ** -0.5, 0.5)
    adjacency = scatter_about(key_of[2], (N_ROW, N_COL, BLK_DEV, BLK, BLK), (BLK_DEV * BLK // NB_DEV) ** -0.5, 0.046875, ((0, 8), (1, 16)))
    row_index = place_ends(jax.random.randint(key_of[3], (N_ROW, N_COL, BLK_DEV), 0, NB_DEV * N_COL), jax.random.fold_in(key_of[3], 1), 0, (NB_DEV * N_COL) - 1).astype(jnp.int32)
    col_index = place_ends(jax.random.randint(key_of[4], (N_ROW, N_COL, BLK_DEV), 0, NB_DEV * N_ROW), jax.random.fold_in(key_of[4], 1), 0, (NB_DEV * N_ROW) - 1).astype(jnp.int32)
    block_count = draw_block_count(jax.random.fold_in(key_of[7], 71), 0)
    grad_out = scatter_about(key_of[6], (NODES, F), 1.0, 6.0, ((0, 128),))
    return {"features": features, "weight": weight, "adjacency": adjacency, "row_index": row_index, "col_index": col_index, "block_count": block_count, "grad_out": grad_out}


def reference(features, weight, adjacency, row_index, col_index, block_count, grad_out):
    nblocks = NODES // BLK
    hidden = jnp.dot(features, weight, preferred_element_type=jnp.float32).astype(jnp.bfloat16)
    hidden = hidden.reshape(nblocks, BLK, F)
    slots = jnp.arange(BLK_DEV, dtype=jnp.int32)
    live = (slots[None, None, :] < block_count[:, :, None]).astype(jnp.float32)
    grows = (jnp.arange(N_ROW, dtype=jnp.int32)[:, None, None] * RB + row_index).astype(jnp.int32)
    gcols = (jnp.arange(N_COL, dtype=jnp.int32)[None, :, None] * CB + col_index).astype(jnp.int32)
    places = N_ROW * N_COL
    items = (adjacency.reshape(places, BLK_DEV, BLK, BLK), grows.reshape(places, BLK_DEV),
             gcols.reshape(places, BLK_DEV), live.reshape(places, BLK_DEV))

    def forward(total, item):
        blocks, brow, bcol, alive = item
        masked = blocks.astype(jnp.float32) * alive[:, None, None]
        picked = hidden[bcol].astype(jnp.float32)
        prods = jnp.einsum('kij,kjf->kif', masked, picked)
        return total.at[brow].add(prods), None

    pre = lax.scan(forward, jnp.zeros((nblocks, BLK, F), jnp.float32), items)[0]
    pre = pre.reshape(NODES, F)
    squash = jnp.tanh(pre)
    activated = squash.astype(jnp.bfloat16)
    slope = (grad_out.astype(jnp.float32) * (1.0 - squash * squash)).astype(jnp.bfloat16)
    slope = slope.reshape(nblocks, BLK, F)

    def backward(total, item):
        blocks, brow, bcol, alive = item
        masked = blocks.astype(jnp.float32) * alive[:, None, None]
        picked = slope[brow].astype(jnp.float32)
        prods = jnp.einsum('kij,kif->kjf', masked, picked)
        return total.at[bcol].add(prods), None

    hidden_grad = lax.scan(backward, jnp.zeros((nblocks, BLK, F), jnp.float32), items)[0]
    hidden_grad_b = hidden_grad.reshape(NODES, F).astype(jnp.bfloat16)
    input_grad = jnp.dot(hidden_grad_b, weight.T, preferred_element_type=jnp.float32).astype(jnp.bfloat16)
    weight_grad = jnp.dot(features.T, hidden_grad_b, preferred_element_type=jnp.float32) * (NODES ** -0.5)
    return activated, input_grad, weight_grad
```

```python
import functools

import jax
import jax.numpy as jnp
from jax import lax
from jax.experimental import pallas as pl
from jax.experimental.pallas import tpu as pltpu
from jax.sharding import PartitionSpec as P

BLK = 128
NX = 4
NZ = 4
NY = 4
ROW_BLOCKS = 64
COL_BLOCKS = 32
CHUNK = 64
UNROLL = 8
F32 = jnp.float32
BF16 = jnp.bfloat16
VMEM_LIMIT = 48 * 1024 * 1024


def vmem_specs(n):
    return [pl.BlockSpec(memory_space=pltpu.VMEM)] * n


def params():
    return pltpu.CompilerParams(vmem_limit_bytes=VMEM_LIMIT)


def start_chunks(adj_ref, buf, sems, nchunks):
    def copy(i):
        return pltpu.make_async_copy(
            adj_ref.at[pl.ds(i * CHUNK, CHUNK)], buf.at[pl.ds(i * CHUNK, CHUNK)], sems.at[i]
        )

    @pl.loop(0, nchunks)
    def _(i):
        copy(i).start()

    return copy


def forward_kernel(nin, nout, target_ref, source_ref, count_ref, adj_ref, *refs):
    ins, outs = refs[:nin], refs[nin : nin + nout]
    buf, feats, acc, sems = refs[nin + nout :]
    live = count_ref[0]
    nchunks = pl.cdiv(live, CHUNK)
    copy = start_chunks(adj_ref, buf, sems, nchunks)
    per = feats.shape[0] // nin
    for i in range(nin):
        feats[pl.ds(i * per, per)] = ins[i][...].reshape(per, BLK, BLK)
    acc[...] = jnp.zeros_like(acc)

    @pl.loop(0, nchunks)
    def _(i):
        copy(i).wait()
        groups = pl.cdiv(jnp.minimum(live - i * CHUNK, CHUNK), UNROLL)

        @pl.loop(0, groups)
        def _(g):
            base = i * CHUNK + g * UNROLL
            prods = [
                jnp.dot(buf[base + j], feats[source_ref[base + j]], preferred_element_type=F32)
                for j in range(UNROLL)
            ]
            for j in range(UNROLL):
                acc[target_ref[base + j]] += prods[j]

    per = ROW_BLOCKS // nout
    for i in range(nout):
        outs[i][...] = acc[pl.ds(i * per, per)].reshape(per * BLK, BLK).astype(outs[i].dtype)


def forward(adjacency, target, source, count, pieces, nout):
    nin = len(pieces)
    rows = ROW_BLOCKS * BLK // nout
    return pl.pallas_call(
        functools.partial(forward_kernel, nin, nout),
        out_shape=[jax.ShapeDtypeStruct((rows, BLK), BF16)] * nout,
        in_specs=[pl.BlockSpec(memory_space=pltpu.SMEM)] * 3
        + [pl.BlockSpec(memory_space=pl.ANY)]
        + vmem_specs(nin),
        out_specs=vmem_specs(nout),
        scratch_shapes=[
            pltpu.VMEM(adjacency.shape, BF16),
            pltpu.VMEM((COL_BLOCKS, BLK, BLK), BF16),
            pltpu.VMEM((ROW_BLOCKS + 1, BLK, BLK), F32),
            pltpu.SemaphoreType.DMA((adjacency.shape[0] // CHUNK,)),
        ],
        compiler_params=params(),
        cost_estimate=pl.CostEstimate(
            flops=2 * 512 * BLK**3 * 4, bytes_accessed=20 * 2**20, transcendentals=0
        ),
        name="sparse_forward",
    )(target, source, count, adjacency, *pieces)


def backward_kernel(nin, target_ref, source_ref, count_ref, adj_ref, *refs):
    ins, (keep, send) = refs[:nin], refs[nin : nin + 2]
    buf, slopes, acc, sems = refs[nin + 2 :]
    live = count_ref[0]
    nchunks = pl.cdiv(live, CHUNK)
    copy = start_chunks(adj_ref, buf, sems, nchunks)
    per = slopes.shape[0] // nin
    for i in range(nin):
        slopes[pl.ds(i * per, per)] = ins[i][...].reshape(per, BLK, BLK)
    acc[...] = jnp.zeros_like(acc)

    @pl.loop(0, nchunks)
    def _(i):
        copy(i).wait()
        groups = pl.cdiv(jnp.minimum(live - i * CHUNK, CHUNK), UNROLL)

        @pl.loop(0, groups)
        def _(g):
            base = i * CHUNK + g * UNROLL
            prods = [
                jnp.dot(slopes[source_ref[base + j]], buf[base + j], preferred_element_type=F32)
                for j in range(UNROLL)
            ]
            for j in range(UNROLL):
                acc[target_ref[base + j]] += prods[j]

    half = COL_BLOCKS // 2
    for b in range(half):
        keep[pl.ds(b * BLK, BLK)] = acc[b].T.astype(keep.dtype)
        send[pl.ds(b * BLK, BLK)] = acc[half + b].T.astype(send.dtype)


def backward(adjacency, target, source, count, pieces):
    nin = len(pieces)
    rows = COL_BLOCKS * BLK // 2
    return pl.pallas_call(
        functools.partial(backward_kernel, nin),
        out_shape=[
            jax.ShapeDtypeStruct((rows, BLK), F32),
            jax.ShapeDtypeStruct((rows, BLK), F32),
        ],
        in_specs=[pl.BlockSpec(memory_space=pltpu.SMEM)] * 3
        + [pl.BlockSpec(memory_space=pl.ANY)]
        + vmem_specs(nin),
        out_specs=vmem_specs(2),
        scratch_shapes=[
            pltpu.VMEM(adjacency.shape, BF16),
            pltpu.VMEM((ROW_BLOCKS, BLK, BLK), BF16),
            pltpu.VMEM((COL_BLOCKS + 1, BLK, BLK), F32),
            pltpu.SemaphoreType.DMA((adjacency.shape[0] // CHUNK,)),
        ],
        compiler_params=params(),
        cost_estimate=pl.CostEstimate(
            flops=2 * 512 * BLK**3 * 4, bytes_accessed=20 * 2**20, transcendentals=0
        ),
        name="sparse_backward",
    )(target, source, count, adjacency, *pieces)


def add_split_kernel(nin, nout, *refs):
    ins, outs = refs[:nin], refs[nin:]
    rows = outs[0].shape[0]
    for i in range(nout):
        total = ins[0][pl.ds(i * rows, rows)].astype(F32)
        for part in ins[1:]:
            total += part[pl.ds(i * rows, rows)].astype(F32)
        outs[i][...] = total.astype(outs[i].dtype)


def add_split(parts, nout, name):
    rows = parts[0].shape[0] // nout
    return pl.pallas_call(
        functools.partial(add_split_kernel, len(parts), nout),
        out_shape=[jax.ShapeDtypeStruct((rows, BLK), F32)]
        + [jax.ShapeDtypeStruct((rows, BLK), BF16)] * (nout - 1),
        in_specs=vmem_specs(len(parts)),
        out_specs=vmem_specs(nout),
        compiler_params=params(),
        name=name,
    )(*parts)


def activate_kernel(weight_ref, grad_ref, *refs):
    first, second = refs[:4], refs[4:8]
    act_ref, slope_ref, total_ref, st_a, st_b = refs[8:]
    half = act_ref.shape[0] // 2
    for i, parts in enumerate((first, second)):
        total_ref[pl.ds(i * half, half)] = (
            parts[0][...] + parts[1][...].astype(F32) + parts[2][...].astype(F32) + parts[3][...].astype(F32)
        )
    pre = jnp.dot(
        total_ref[...], weight_ref[...].astype(F32), precision=lax.Precision.HIGHEST, preferred_element_type=F32
    )
    squash = jnp.tanh(pre)
    act_ref[...] = squash.astype(BF16)
    slope = (grad_ref[...].astype(F32) * (1.0 - squash * squash)).astype(BF16)
    slope_ref[...] = slope
    for i, out in enumerate((st_a, st_b)):
        for b in range(half // BLK):
            out[pl.ds(b * BLK, BLK)] = slope[i * half + b * BLK : i * half + (b + 1) * BLK].T


def activate(weight, grad_out, first, second):
    rows = grad_out.shape[0]
    return pl.pallas_call(
        activate_kernel,
        out_shape=[
            jax.ShapeDtypeStruct((rows, BLK), BF16),
            jax.ShapeDtypeStruct((rows, BLK), BF16),
            jax.ShapeDtypeStruct((rows, BLK), F32),
            jax.ShapeDtypeStruct((rows // 2, BLK), BF16),
            jax.ShapeDtypeStruct((rows // 2, BLK), BF16),
        ],
        in_specs=vmem_specs(10),
        out_specs=vmem_specs(5),
        compiler_params=params(),
        name="activate",
    )(weight, grad_out, *first, *second)


def finish_kernel(weight_ref, *refs):
    parts, out_ref = refs[:4], refs[4]
    total = parts[0][...]
    for part in parts[1:]:
        total += part[...].astype(F32)
    out_ref[...] = lax.dot_general(
        total.astype(BF16), weight_ref[...], (((1,), (1,)), ((), ())), preferred_element_type=F32
    ).astype(BF16)


def finish(weight, parts):
    return pl.pallas_call(
        finish_kernel,
        out_shape=jax.ShapeDtypeStruct(parts[0].shape, BF16),
        in_specs=vmem_specs(5),
        out_specs=pl.BlockSpec(memory_space=pltpu.VMEM),
        compiler_params=params(),
        name="finish",
    )(weight, *parts)


def shift_x(a, d):
    return lax.ppermute(a, "col", [(i, (i // NZ + d) % NX * NZ + i % NZ) for i in range(NX * NZ)])


def shift_z(a, d):
    return lax.ppermute(a, "col", [(i, i // NZ * NZ + (i % NZ + d) % NZ) for i in range(NX * NZ)])


def shift_y(a, d):
    return lax.ppermute(a, "row", [(i, (i // 2 + d) % NY * 2 + i % 2) for i in range(NY * 2)])


def swap_core(a):
    return lax.ppermute(a, "row", [(i, i ^ 1) for i in range(NY * 2)])


def sum_along(shift, a, n):
    return a + sum(shift(a, d) for d in range(1, n))


def local(features, weight, adjacency, row_index, col_index, block_count, grad_out):
    row, col = lax.axis_index("row"), lax.axis_index("col")
    y, core = row // 2, row % 2
    x, z = col // NZ, col % NZ
    blocks = adjacency[0, 0]
    count = block_count[0]
    alive = jnp.arange(blocks.shape[0], dtype=jnp.int32) < count[0]
    brow, bcol = row_index[0, 0], col_index[0, 0]

    rx, rz, rb = brow // 16, brow // 4 % 4, brow % 4
    cy, cc, cb = bcol // 8, bcol // 4 % 2, bcol % 4
    ex, gz = (rx - x) % NX, (rz - z) % NZ
    to_row = jnp.where(rb < 2, ex * 8 + gz * 2 + rb, 32 + gz * 8 + ex * 2 + rb - 2)
    to_row = jnp.where(alive, to_row, ROW_BLOCKS)
    ex, gz = (x - rx) % NX, (z - rz) % NZ
    from_row = jnp.where(rb < 2, gz * 8 + ex * 2 + rb, 32 + ex * 8 + gz * 2 + rb - 2)
    from_row = jnp.where(alive, from_row, 0)
    other = cc ^ core
    to_col = jnp.where(alive, other * 16 + (cy - y) % NY * 4 + cb, COL_BLOCKS)
    from_col = jnp.where(alive, other * 16 + (y - cy) % NY * 4 + cb, 0)

    mine = [features] + [shift_y(features, d) for d in range(1, NY)]
    theirs = [swap_core(a) for a in mine]

    parts = forward(blocks, to_row, from_col, count, mine + theirs, 8)
    first = [parts[0]] + [shift_x(parts[d], d) for d in range(1, NX)]
    second = [parts[4]] + [shift_z(parts[4 + d], d) for d in range(1, NZ)]
    first = add_split(first, NZ, "add_x")
    second = add_split(second, NX, "add_z")
    first = [first[0]] + [shift_z(first[d], d) for d in range(1, NZ)]
    second = [second[0]] + [shift_x(second[d], d) for d in range(1, NX)]
    activated, slope, total, slope_a, slope_b = activate(weight, grad_out, first, second)

    slope_a = jnp.concatenate([slope_a] + [shift_x(slope_a, d) for d in range(1, NX)])
    slope_b = jnp.concatenate([slope_b] + [shift_z(slope_b, d) for d in range(1, NZ)])
    slopes = [slope_a] + [shift_z(slope_a, d) for d in range(1, NZ)]
    slopes += [slope_b] + [shift_x(slope_b, d) for d in range(1, NX)]

    term = lax.dot_general(
        total, slope.astype(F32), (((0,), (0,)), ((), ())), precision=lax.Precision.HIGHEST, preferred_element_type=F32
    )
    term = term + swap_core(term)
    term = sum_along(shift_y, term, NY)
    term = sum_along(shift_x, term, NX)
    term = sum_along(shift_z, term, NZ)
    nodes_all = features.shape[0] * lax.axis_size("row") * lax.axis_size("col")
    weight_grad = term * nodes_all ** (-0.5)

    keep, send = backward(blocks, to_col, from_row, count, slopes)
    parts = add_split([keep, swap_core(send)], NY, "add_core")
    parts = [parts[0]] + [shift_y(parts[d], d) for d in range(1, NY)]
    input_grad = finish(weight, parts)
    return (activated, input_grad, weight_grad)


def solution(mesh):
    placed = (
        P(("col", "row"), None),
        P(),
        P("row", "col", None, None, None),
        P("row", "col", None),
        P("row", "col", None),
        P("row", "col"),
        P(("row", "col"), None),
    )
    return jax.shard_map(
        local,
        mesh=mesh,
        in_specs=placed,
        out_specs=(P(("row", "col"), None), P(("col", "row"), None), P()),
        check_vma=False,
    )
```

```python
import functools

import jax
import jax.numpy as jnp
from jax import lax
from jax.experimental import pallas as pl
from jax.experimental.pallas import tpu as pltpu
from jax.sharding import PartitionSpec as P

BLK = 128
NX = 4
NZ = 4
NY = 4
ROW_BLOCKS = 64
COL_BLOCKS = 32
HALF = 32
OWN = 4
UNROLL = 64
F32 = jnp.float32
BF16 = jnp.bfloat16
VMEM_LIMIT = 24 * 1024 * 1024


def vmem_specs(n):
    return [pl.BlockSpec(memory_space=pltpu.VMEM)] * n


def params():
    return pltpu.CompilerParams(vmem_limit_bytes=VMEM_LIMIT)


def accumulate(live, codes_ref, acc, product):
    @pl.loop(0, pl.cdiv(live, UNROLL))
    def _(g):
        codes = [codes_ref[g * UNROLL + j] for j in range(UNROLL)]
        prods = [product(c & 511, c >> 16) for c in codes]
        for j in range(UNROLL):
            acc[(codes[j] >> 9) & 127] += prods[j]


def sparse_cost():
    return pl.CostEstimate(flops=512 * BLK**3 * 4, bytes_accessed=10 * 2**20, transcendentals=0)


def load_kernel(adj_ref, out_ref, sem):
    copy = pltpu.make_async_copy(adj_ref, out_ref, sem)
    copy.start()
    copy.wait()


def load(adjacency):
    return pl.pallas_call(
        load_kernel,
        out_shape=jax.ShapeDtypeStruct(adjacency.shape, adjacency.dtype),
        in_specs=[pl.BlockSpec(memory_space=pl.ANY)],
        out_specs=pl.BlockSpec(memory_space=pltpu.VMEM),
        scratch_shapes=[pltpu.SemaphoreType.DMA],
        compiler_params=params(),
        cost_estimate=pl.CostEstimate(flops=0, bytes_accessed=2 * adjacency.size * 2, transcendentals=0),
        name="load_blocks",
    )(adjacency)


def forward_kernel(nin, codes_ref, count_ref, adj_ref, *refs):
    ins, outs = refs[:nin], refs[nin:-2]
    feats, acc = refs[-2:]
    per = feats.shape[0] // nin
    for i in range(nin):
        feats[pl.ds(i * per, per)] = ins[i][...].reshape(per, BLK, BLK)
    acc[...] = jnp.zeros_like(acc)

    def product(slot, source):
        return jnp.dot(adj_ref[slot], feats[source], preferred_element_type=F32)

    accumulate(count_ref[0], codes_ref, acc, product)
    at = 0
    for out in outs:
        blocks = out.shape[0] // BLK
        out[...] = acc[pl.ds(at, blocks)].reshape(out.shape).astype(out.dtype)
        at += blocks


def forward(adjacency, codes, count, pieces, outs, name):
    return pl.pallas_call(
        functools.partial(forward_kernel, len(pieces)),
        out_shape=[jax.ShapeDtypeStruct((units * OWN * BLK, BLK), dtype) for units, dtype in outs],
        in_specs=[pl.BlockSpec(memory_space=pltpu.SMEM)] * 2 + vmem_specs(1 + len(pieces)),
        out_specs=vmem_specs(len(outs)),
        scratch_shapes=[
            pltpu.VMEM((COL_BLOCKS, BLK, BLK), BF16),
            pltpu.VMEM((HALF + 1, BLK, BLK), F32),
        ],
        compiler_params=params(),
        cost_estimate=sparse_cost(),
        name=name,
    )(codes, count, adjacency, *pieces)


def gather_slopes(slopes, ins):
    at = 0
    for part in ins:
        blocks = part.shape[0] // BLK - 1
        slopes[pl.ds(at, blocks)] = part[pl.ds(0, blocks * BLK)].reshape(blocks, BLK, BLK)
        at += blocks


def last_block(part):
    return part[pl.ds(part.shape[0] - BLK, BLK)].astype(F32)


def backward_even_kernel(nin, codes_ref, count_ref, adj_ref, *refs):
    ins, (acc, wsum) = refs[:nin], refs[nin : nin + 2]
    slopes = refs[-1]
    gather_slopes(slopes, ins)
    acc[...] = jnp.zeros_like(acc)

    def product(slot, source):
        return jnp.dot(slopes[source], adj_ref[slot], preferred_element_type=F32)

    accumulate(count_ref[0], codes_ref, acc, product)
    wsum[...] = sum(last_block(part) for part in ins)


def backward_even(adjacency, codes, count, pieces):
    return pl.pallas_call(
        functools.partial(backward_even_kernel, len(pieces)),
        out_shape=[
            jax.ShapeDtypeStruct((COL_BLOCKS + 1, BLK, BLK), F32),
            jax.ShapeDtypeStruct((BLK, BLK), F32),
        ],
        in_specs=[pl.BlockSpec(memory_space=pltpu.SMEM)] * 2 + vmem_specs(1 + len(pieces)),
        out_specs=vmem_specs(2),
        scratch_shapes=[pltpu.VMEM((HALF, BLK, BLK), BF16)],
        compiler_params=params(),
        cost_estimate=sparse_cost(),
        name="backward_even",
    )(codes, count, adjacency, *pieces)


def backward_odd_kernel(nin, codes_ref, count_ref, adj_ref, part_ref, wpart_ref, *refs):
    ins, (keep, send, wsum) = refs[:nin], refs[nin : nin + 3]
    slopes, acc = refs[nin + 3 :]
    gather_slopes(slopes, ins)
    acc[...] = part_ref[...]

    def product(slot, source):
        return jnp.dot(slopes[source], adj_ref[slot], preferred_element_type=F32)

    accumulate(count_ref[0], codes_ref, acc, product)
    half = COL_BLOCKS // 2
    for b in range(half):
        keep[pl.ds(b * BLK, BLK)] = acc[b].T.astype(keep.dtype)
        send[pl.ds(b * BLK, BLK)] = acc[half + b].T.astype(send.dtype)
    total = wpart_ref[...] + sum(last_block(part) for part in ins)
    wsum[...] = total
    send[pl.ds(half * BLK, BLK)] = total.astype(send.dtype)


def backward_odd(adjacency, codes, count, part, wpart, pieces):
    rows = COL_BLOCKS * BLK // 2
    return pl.pallas_call(
        functools.partial(backward_odd_kernel, len(pieces)),
        out_shape=[
            jax.ShapeDtypeStruct((rows, BLK), F32),
            jax.ShapeDtypeStruct((rows + BLK, BLK), F32),
            jax.ShapeDtypeStruct((BLK, BLK), F32),
        ],
        in_specs=[pl.BlockSpec(memory_space=pltpu.SMEM)] * 2 + vmem_specs(3 + len(pieces)),
        out_specs=vmem_specs(3),
        scratch_shapes=[
            pltpu.VMEM((HALF, BLK, BLK), BF16),
            pltpu.VMEM((COL_BLOCKS + 1, BLK, BLK), F32),
        ],
        compiler_params=params(),
        cost_estimate=sparse_cost(),
        name="backward_odd",
    )(codes, count, adjacency, part, wpart, *pieces)


def add_split_kernel(nin, *refs):
    ins, outs = refs[:nin], refs[nin:]
    at = 0
    for out in outs:
        rows = out.shape[0]
        total = ins[0][pl.ds(at, rows)].astype(F32)
        for part in ins[1:]:
            total += part[pl.ds(at, rows)].astype(F32)
        out[...] = total.astype(out.dtype)
        at += rows


def add_split(parts, dtypes, name):
    rows = parts[0].shape[0] // len(dtypes)
    return pl.pallas_call(
        functools.partial(add_split_kernel, len(parts)),
        out_shape=[jax.ShapeDtypeStruct((rows, BLK), dtype) for dtype in dtypes],
        in_specs=vmem_specs(len(parts)),
        out_specs=vmem_specs(len(dtypes)),
        compiler_params=params(),
        name=name,
    )(*parts)


def activate_kernel(weight_ref, grad_ref, *refs):
    parts, (act_ref, pay_ref) = refs[:-2], refs[-2:]
    rows = act_ref.shape[0]
    total = parts[0][...]
    for part in parts[1:]:
        total += part[...].astype(F32)
    weight = weight_ref[...].astype(F32)
    pre = jnp.dot(total, weight, precision=lax.Precision.HIGHEST, preferred_element_type=F32)
    squash = jnp.tanh(pre)
    act_ref[...] = squash.astype(BF16)
    slope = (grad_ref[...].astype(F32) * (1.0 - squash * squash)).astype(BF16)
    high = total.astype(BF16)
    low = (total - high.astype(F32)).astype(BF16)
    wterm = jnp.zeros((BLK, BLK), F32)
    for b in range(0, rows, BLK):
        turned = slope[b : b + BLK].T
        pay_ref[pl.ds(b, BLK)] = turned
        wterm += jnp.dot(turned, high[b : b + BLK], preferred_element_type=F32)
        wterm += jnp.dot(turned, low[b : b + BLK], preferred_element_type=F32)
    pay_ref[pl.ds(rows, BLK)] = wterm.astype(BF16)


def activate(weight, grad_out, parts):
    rows = grad_out.shape[0]
    return pl.pallas_call(
        activate_kernel,
        out_shape=[
            jax.ShapeDtypeStruct((rows, BLK), BF16),
            jax.ShapeDtypeStruct((rows + BLK, BLK), BF16),
        ],
        in_specs=vmem_specs(2 + len(parts)),
        out_specs=vmem_specs(2),
        compiler_params=params(),
        name="activate",
    )(weight, grad_out, *parts)


def merge_kernel(*refs):
    parts, out = refs[:-1], refs[-1]
    rows = parts[0].shape[0] - BLK
    total = jnp.zeros((BLK, BLK), F32)
    for i, part in enumerate(parts):
        out[pl.ds(i * rows, rows)] = part[pl.ds(0, rows)]
        total += last_block(part)
    out[pl.ds(len(parts) * rows, BLK)] = total.astype(BF16)


def merge(parts, name):
    rows = len(parts) * (parts[0].shape[0] - BLK) + BLK
    return pl.pallas_call(
        merge_kernel,
        out_shape=jax.ShapeDtypeStruct((rows, BLK), BF16),
        in_specs=vmem_specs(len(parts)),
        out_specs=pl.BlockSpec(memory_space=pltpu.VMEM),
        compiler_params=params(),
        name=name,
    )(*parts)


def add_core_kernel(nout, keep, wkeep, got, *outs):
    rows = keep.shape[0] // nout
    wsum = wkeep[...] + got[pl.ds(rows * nout, BLK)].astype(F32)
    outs[nout][...] = wsum
    for i in range(nout):
        total = keep[pl.ds(i * rows, rows)] + got[pl.ds(i * rows, rows)].astype(F32)
        outs[i][pl.ds(0, rows)] = total.astype(outs[i].dtype)
        if i:
            outs[i][pl.ds(rows, BLK)] = wsum.astype(outs[i].dtype)


def add_core(keep, wkeep, got):
    rows = keep.shape[0] // NY
    return pl.pallas_call(
        functools.partial(add_core_kernel, NY),
        out_shape=[jax.ShapeDtypeStruct((rows, BLK), F32)]
        + [jax.ShapeDtypeStruct((rows + BLK, BLK), BF16)] * (NY - 1)
        + [jax.ShapeDtypeStruct((BLK, BLK), F32)],
        in_specs=vmem_specs(3),
        out_specs=vmem_specs(NY + 1),
        compiler_params=params(),
        name="add_core",
    )(keep, wkeep, got)


def finish_kernel(scale, weight_ref, own, wown, *refs):
    parts, (out_ref, wout_ref) = refs[:-2], refs[-2:]
    rows = own.shape[0]
    total, wsum = own[...], wown[...]
    for part in parts:
        total += part[pl.ds(0, rows)].astype(F32)
        wsum += part[pl.ds(rows, BLK)].astype(F32)
    out_ref[...] = lax.dot_general(
        total.astype(BF16), weight_ref[...], (((1,), (1,)), ((), ())), preferred_element_type=F32
    ).astype(BF16)
    wout_ref[...] = wsum.T * scale


def finish(scale, weight, own, wown, parts):
    return pl.pallas_call(
        functools.partial(finish_kernel, scale),
        out_shape=[
            jax.ShapeDtypeStruct(own.shape, BF16),
            jax.ShapeDtypeStruct((BLK, BLK), F32),
        ],
        in_specs=vmem_specs(3 + len(parts)),
        out_specs=vmem_specs(2),
        compiler_params=params(),
        name="finish",
    )(weight, own, wown, *parts)


def shift_x(a, d):
    return lax.ppermute(a, "col", [(i, (i // NZ + d) % NX * NZ + i % NZ) for i in range(NX * NZ)])


def shift_z(a, d):
    return lax.ppermute(a, "col", [(i, i // NZ * NZ + (i % NZ + d) % NZ) for i in range(NX * NZ)])


def shift_y(a, d):
    return lax.ppermute(a, "row", [(i, (i // 2 + d) % NY * 2 + i % 2) for i in range(NY * 2)])


def swap_core(a):
    return lax.ppermute(a, "row", [(i, i ^ 1) for i in range(NY * 2)])


def order_slots(slots, odd, even, forward_code, backward_code, idle_forward, idle_backward):
    before = slots[:, None] >= slots[None, :]
    rank_odd = jnp.sum(before & odd[None, :], axis=1, dtype=jnp.int32) - 1
    rank_even = jnp.sum(before & even[None, :], axis=1, dtype=jnp.int32) - 1
    lists = []
    for chosen, rank in ((odd, rank_odd), (even, rank_even)):
        here = (slots[:, None] == rank[None, :]) & chosen[None, :]
        count = jnp.sum(chosen, dtype=jnp.int32)
        lists.append(count[None])
        for code, idle in ((forward_code, idle_forward), (backward_code, idle_backward)):
            picked = jnp.sum(jnp.where(here, code[None, :], 0), axis=1, dtype=jnp.int32)
            lists.append(jnp.where(slots < count, picked, idle))
    return lists


def local(features, weight, adjacency, row_index, col_index, block_count, grad_out):
    row, col = lax.axis_index("row"), lax.axis_index("col")
    y, core = row // 2, row % 2
    x, z = col // NZ, col % NZ
    capacity = adjacency.shape[2]
    slots = jnp.arange(capacity, dtype=jnp.int32)
    alive = slots < block_count[0, 0]
    brow, bcol = row_index[0, 0], col_index[0, 0]

    mine = [features] + [shift_y(features, d) for d in range(1, NY)]
    theirs = [swap_core(a) for a in mine]
    blocks = load(adjacency[0, 0])

    rx, rz, rb = brow // 16, brow // 4 % 4, brow % 4
    cy, cc, cb = bcol // 8, bcol // 4 % 2, bcol % 4
    odd = alive & ((rx - x) % 2 == 1)
    even = alive & ((rx - x) % 2 == 0)
    to_row = (rx - x) % NX // 2 * 16 + (rz - z) % NZ * OWN + rb
    from_row = (x - rx) % NX // 2 * 16 + (z - rz) % NZ * OWN + rb
    to_col = (cc ^ core) * 16 + (cy - y) % NY * OWN + cb
    from_col = (cc ^ core) * 16 + (y - cy) % NY * OWN + cb
    n_odd, odd_forward, odd_backward, n_even, even_forward, even_backward = order_slots(
        slots,
        odd,
        even,
        slots + 512 * to_row + 65536 * from_col,
        slots + 512 * to_col + 65536 * from_row,
        512 * HALF,
        512 * COL_BLOCKS,
    )

    x1, x3 = forward(blocks, odd_forward, n_odd, mine + theirs, [(4, BF16)] * 2, "forward_odd")
    column, across, z1, z2, z3 = forward(
        blocks, even_forward, n_even, mine + theirs, [(4, F32), (1, F32)] + [(1, BF16)] * 3, "forward_even"
    )
    x1, x3 = shift_x(x1, 1), shift_x(x3, 3)
    z1, z2, z3 = shift_z(z1, 1), shift_z(z2, 2), shift_z(z3, 3)
    across = add_split([across, z1, z2, z3], [BF16], "add_z")[0]
    own, z1, z2, z3 = add_split([column, x1, x3], [F32, BF16, BF16, BF16], "add_x")
    parts = [own, shift_z(z1, 1), shift_z(z2, 2), shift_z(z3, 3), shift_x(across, 2)]
    activated, pay = activate(weight, grad_out, parts)

    beside = [shift_z(pay, d) for d in range(1, NZ)]
    across = shift_x(pay, 2)
    column = merge([pay] + beside, "merge_z")
    odds = [shift_x(column, 1), shift_x(column, 3)]
    evens = [column, across] + [shift_z(across, d) for d in range(1, NZ)]

    part, wpart = backward_even(blocks, even_backward, n_even, evens)
    keep, send, wkeep = backward_odd(blocks, odd_backward, n_odd, part, wpart, odds)
    parts = add_core(keep, wkeep, swap_core(send))
    got = [shift_y(parts[d], d) for d in range(1, NY)]
    nodes_all = features.shape[0] * lax.axis_size("row") * lax.axis_size("col")
    input_grad, weight_grad = finish(nodes_all ** (-0.5), weight, parts[0], parts[NY], got)
    return (activated, input_grad, weight_grad)


def solution(mesh):
    placed = (
        P(("col", "row"), None),
        P(),
        P("row", "col", None, None, None),
        P("row", "col", None),
        P("row", "col", None),
        P("row", "col"),
        P(("row", "col"), None),
    )
    return jax.shard_map(
        local,
        mesh=mesh,
        in_specs=placed,
        out_specs=(P(("row", "col"), None), P(("col", "row"), None), P()),
        check_vma=False,
    )
```

```python
import functools

import jax
import jax.numpy as jnp
from jax import lax
from jax.experimental import pallas as pl
from jax.experimental.pallas import tpu as pltpu
from jax.sharding import PartitionSpec as P

BLK = 128
NX = 4
NZ = 4
NY = 4
ROW_BLOCKS = 64
COL_BLOCKS = 32
HALF = 32
OWN = 4
F32 = jnp.float32
BF16 = jnp.bfloat16
VMEM_LIMIT = 24 * 1024 * 1024


def vmem_specs(n):
    return [pl.BlockSpec(memory_space=pltpu.VMEM)] * n


def params():
    return pltpu.CompilerParams(vmem_limit_bytes=VMEM_LIMIT)


ODD_F, TWO_F, ZERO_F, ZERO_B, TWO_B, OTHER_B, OWN_B = range(7)
LISTS = 8


def prepare_kernel(count_ref, brow_hbm, bcol_hbm, adj_ref, blocks_ref, codes_ref, brow_ref, bcol_ref, sems):
    first = pltpu.make_async_copy(brow_hbm, brow_ref, sems.at[0])
    second = pltpu.make_async_copy(bcol_hbm, bcol_ref, sems.at[1])
    copy = pltpu.make_async_copy(adj_ref, blocks_ref, sems.at[2])
    first.start()
    second.start()
    copy.start()
    first.wait()
    second.wait()
    row, col = lax.axis_index("row"), lax.axis_index("col")
    y, core = row >> 1, row & 1
    x, z = col >> 2, col & 3
    brow, bcol = brow_ref[...], bcol_ref[...]
    capacity = brow.shape[1]
    slot = lax.broadcasted_iota(jnp.int32, (1, capacity), 1)
    alive = slot < count_ref[0, 0]
    rx, rz, rb = (brow >> 4) & 3, (brow >> 2) & 3, brow & 3
    cy, cc, cb = (bcol >> 3) & 3, (bcol >> 2) & 1, bcol & 3
    ahead, behind = (rx - x) & 3, (x - rx) & 3
    other = cc ^ core
    odd = ahead & 1
    to_row = odd * (ahead >> 1) * 16 + ((rz - z) & 3) * OWN + rb
    from_row = odd * (behind >> 1) * 16 + ((z - rz) & 3) * OWN + rb
    to_col = (1 - odd) * other * 16 + ((cy - y) & 3) * OWN + cb
    from_col = other * 16 + ((y - cy) & 3) * OWN + cb
    kind = jnp.where(odd == 1, 2 + (1 - other), ahead >> 1)
    kind = jnp.where(alive, kind, 4)
    row_codes = [
        (slot + 512 * to_row + 65536 * from_col).astype(F32),
        (slot + 512 * to_col + 65536 * from_row).astype(F32),
        kind.astype(F32),
    ]
    counts = [jnp.sum((kind == k).astype(F32), axis=1, keepdims=True) for k in range(4)]
    member = [(kind == k).astype(F32) for k in range(4)]
    lists = [jnp.zeros((1, capacity), F32) for _ in range(7)]
    step = 64
    lane = lax.broadcasted_iota(jnp.int32, (step, capacity), 1)
    place = lane.astype(F32)
    for c in range(0, capacity, step):
        sub = lax.broadcasted_iota(jnp.int32, (step, capacity), 0) + c
        fcode, bcode, ckind = (
            jnp.sum(jnp.where(lane == sub, v, 0.0), axis=1, keepdims=True) for v in row_codes
        )
        ranks = [
            jnp.sum(jnp.where(lane <= sub, m, 0.0), axis=1, keepdims=True) - 1.0 for m in member
        ]
        ranks = [jnp.where(ckind == float(k), r, -1.0) for k, r in enumerate(ranks)]
        both = jnp.where(ckind == 2.0, ranks[2], jnp.where(ckind == 3.0, ranks[3] + counts[2], -1.0))
        for q, rank, code in (
            (ODD_F, both, fcode),
            (TWO_F, ranks[1], fcode),
            (ZERO_F, ranks[0], fcode),
            (ZERO_B, ranks[0], bcode),
            (TWO_B, ranks[1], bcode),
            (OTHER_B, ranks[2], bcode),
            (OWN_B, ranks[3], bcode),
        ):
            lists[q] += jnp.sum(jnp.where(place == rank, code, 0.0), axis=0, keepdims=True)
    where = slot.astype(F32)
    codes_ref[...] = jnp.zeros_like(codes_ref)
    for q, count, idle in (
        (ODD_F, counts[2] + counts[3], HALF),
        (TWO_F, counts[1], HALF // 2),
        (ZERO_F, counts[0], HALF // 2),
        (ZERO_B, counts[0], COL_BLOCKS),
        (TWO_B, counts[1], COL_BLOCKS),
        (OTHER_B, counts[2], COL_BLOCKS // 2),
        (OWN_B, counts[3], COL_BLOCKS // 2),
    ):
        codes_ref[q : q + 1, 0:capacity] = jnp.where(where < count, lists[q], 512.0 * idle).astype(jnp.int32)
        codes_ref[q : q + 1, capacity : capacity + BLK] = jnp.broadcast_to(count, (1, BLK)).astype(jnp.int32)
    copy.wait()


def prepare(adjacency, row_index, col_index, block_count):
    capacity = adjacency.shape[0]
    return pl.pallas_call(
        prepare_kernel,
        out_shape=[
            jax.ShapeDtypeStruct(adjacency.shape, adjacency.dtype),
            jax.ShapeDtypeStruct((LISTS, capacity + BLK), jnp.int32),
        ],
        in_specs=[pl.BlockSpec(memory_space=pltpu.SMEM)] + [pl.BlockSpec(memory_space=pltpu.HBM)] * 3,
        out_specs=vmem_specs(2),
        scratch_shapes=[pltpu.VMEM((1, capacity), jnp.int32)] * 2 + [pltpu.SemaphoreType.DMA((3,))],
        compiler_params=params(),
        cost_estimate=pl.CostEstimate(flops=0, bytes_accessed=2 * adjacency.size * 2, transcendentals=0),
        name="prepare",
    )(block_count, row_index, col_index, adjacency)


def accumulate(which, unroll, codes_ref, acc, product):
    live = codes_ref[which, codes_ref.shape[1] - BLK]

    @pl.loop(0, (live + unroll - 1) // unroll)
    def _(g):
        codes = [codes_ref[which, g * unroll + j] for j in range(unroll)]
        prods = [product(c & 511, c >> 16) for c in codes]
        for j in range(unroll):
            acc[(codes[j] >> 9) & 127] += prods[j]


def sparse_cost(share):
    return pl.CostEstimate(
        flops=int(512 * BLK**3 * 8 * share), bytes_accessed=int(20 * 2**20 * share), transcendentals=0
    )


def sparse_call(kernel, codes, adjacency, operands, outs, scratch, share, name):
    return pl.pallas_call(
        kernel,
        out_shape=[jax.ShapeDtypeStruct(shape, dtype) for shape, dtype in outs],
        in_specs=[pl.BlockSpec(memory_space=pltpu.SMEM)] + vmem_specs(1 + len(operands)),
        out_specs=vmem_specs(len(outs)),
        scratch_shapes=[pltpu.VMEM((blocks, BLK, BLK), dtype) for blocks, dtype in scratch],
        compiler_params=params(),
        cost_estimate=sparse_cost(share),
        name=name,
    )(codes, adjacency, *operands)


def write_rows(acc, outs):
    at = 0
    for out in outs:
        blocks = out.shape[0] // BLK
        out[...] = acc[pl.ds(at, blocks)].reshape(out.shape).astype(out.dtype)
        at += blocks


def forward_odd_kernel(nin, codes_ref, adj_ref, *refs):
    ins, (feats, *outs), acc = refs[:nin], refs[nin:-1], refs[-1]
    per = feats.shape[0] // nin
    for i in range(nin):
        feats[pl.ds(i * per, per)] = ins[i][...].reshape(per, BLK, BLK)
    acc[...] = jnp.zeros_like(acc)

    def product(slot, source):
        return jnp.dot(adj_ref[slot], feats[source], preferred_element_type=F32)

    accumulate(ODD_F, 64, codes_ref, acc, product)
    write_rows(acc, outs)


def forward_even_kernel(which, codes_ref, adj_ref, feats, *refs):
    outs, acc = refs[:-1], refs[-1]
    acc[...] = jnp.zeros_like(acc)

    def product(slot, source):
        return jnp.dot(adj_ref[slot], feats[source], preferred_element_type=F32)

    accumulate(which, 32, codes_ref, acc, product)
    write_rows(acc, outs)


def gather_slopes(slopes, ins):
    at = 0
    for part in ins:
        blocks = part.shape[0] // BLK - 1
        slopes[pl.ds(at, blocks)] = part[pl.ds(0, blocks * BLK)].reshape(blocks, BLK, BLK)
        at += blocks


def last_block(part):
    return part[pl.ds(part.shape[0] - BLK, BLK)].astype(F32)


def backward_zero_kernel(codes_ref, adj_ref, column, acc, slopes):
    gather_slopes(slopes, [column])
    acc[...] = jnp.zeros_like(acc)

    def product(slot, source):
        return jnp.dot(slopes[source], adj_ref[slot], preferred_element_type=F32)

    accumulate(ZERO_B, 32, codes_ref, acc, product)


def backward_two_kernel(nin, codes_ref, adj_ref, before, column, *refs):
    ins, (acc, wsum), slopes = refs[:nin], refs[nin : nin + 2], refs[-1]
    gather_slopes(slopes, ins)
    acc[...] = before[...]

    def product(slot, source):
        return jnp.dot(slopes[source], adj_ref[slot], preferred_element_type=F32)

    accumulate(TWO_B, 32, codes_ref, acc, product)
    wsum[...] = last_block(column) + sum(last_block(part) for part in ins)


def backward_other_kernel(codes_ref, adj_ref, before, wpart, first, second, send, wsum, slopes, acc):
    half = COL_BLOCKS // 2
    gather_slopes(slopes, [first, second])
    acc[...] = before[pl.ds(half, half + 1)]

    def product(slot, source):
        return jnp.dot(slopes[source], adj_ref[slot], preferred_element_type=F32)

    accumulate(OTHER_B, 32, codes_ref, acc, product)
    for b in range(half):
        send[pl.ds(b * BLK, BLK)] = acc[b].T
    total = wpart[...] + last_block(first) + last_block(second)
    wsum[...] = total
    send[pl.ds(half * BLK, BLK)] = total


def backward_own_kernel(codes_ref, adj_ref, before, first, second, keep, slopes, acc):
    half = COL_BLOCKS // 2
    gather_slopes(slopes, [first, second])
    acc[...] = before[pl.ds(0, half + 1)]

    def product(slot, source):
        return jnp.dot(slopes[source], adj_ref[slot], preferred_element_type=F32)

    accumulate(OWN_B, 32, codes_ref, acc, product)
    for b in range(half):
        keep[pl.ds(b * BLK, BLK)] = acc[b].T


def add_split_kernel(nin, *refs):
    ins, outs = refs[:nin], refs[nin:]
    at = 0
    for out in outs:
        rows = out.shape[0]
        total = ins[0][pl.ds(at, rows)].astype(F32)
        for part in ins[1:]:
            total += part[pl.ds(at, rows)].astype(F32)
        out[...] = total.astype(out.dtype)
        at += rows


def add_split(parts, dtypes, name):
    rows = parts[0].shape[0] // len(dtypes)
    return pl.pallas_call(
        functools.partial(add_split_kernel, len(parts)),
        out_shape=[jax.ShapeDtypeStruct((rows, BLK), dtype) for dtype in dtypes],
        in_specs=vmem_specs(len(parts)),
        out_specs=vmem_specs(len(dtypes)),
        compiler_params=params(),
        name=name,
    )(*parts)


def activate_kernel(weight_ref, grad_ref, *refs):
    parts, (act_ref, pay_ref) = refs[:-2], refs[-2:]
    rows = act_ref.shape[0]
    total = parts[0][...]
    for part in parts[1:]:
        total += part[...].astype(F32)
    weight = weight_ref[...].astype(F32)
    pre = jnp.dot(total, weight, precision=lax.Precision.HIGHEST, preferred_element_type=F32)
    squash = jnp.tanh(pre)
    act_ref[...] = squash.astype(BF16)
    slope = (grad_ref[...].astype(F32) * (1.0 - squash * squash)).astype(BF16)
    high = total.astype(BF16)
    low = (total - high.astype(F32)).astype(BF16)
    wterm = jnp.zeros((BLK, BLK), F32)
    for b in range(0, rows, BLK):
        turned = slope[b : b + BLK].T
        pay_ref[pl.ds(b, BLK)] = turned
        wterm += jnp.dot(turned, high[b : b + BLK], preferred_element_type=F32)
        wterm += jnp.dot(turned, low[b : b + BLK], preferred_element_type=F32)
    pay_ref[pl.ds(rows, BLK)] = wterm.astype(BF16)


def activate(weight, grad_out, parts):
    rows = grad_out.shape[0]
    return pl.pallas_call(
        activate_kernel,
        out_shape=[
            jax.ShapeDtypeStruct((rows, BLK), BF16),
            jax.ShapeDtypeStruct((rows + BLK, BLK), BF16),
        ],
        in_specs=vmem_specs(2 + len(parts)),
        out_specs=vmem_specs(2),
        compiler_params=params(),
        name="activate",
    )(weight, grad_out, *parts)


def merge_kernel(*refs):
    parts, out = refs[:-1], refs[-1]
    rows = parts[0].shape[0] - BLK
    total = jnp.zeros((BLK, BLK), F32)
    for i, part in enumerate(parts):
        out[pl.ds(i * rows, rows)] = part[pl.ds(0, rows)]
        total += last_block(part)
    out[pl.ds(len(parts) * rows, BLK)] = total.astype(BF16)


def merge(parts, name):
    rows = len(parts) * (parts[0].shape[0] - BLK) + BLK
    return pl.pallas_call(
        merge_kernel,
        out_shape=jax.ShapeDtypeStruct((rows, BLK), BF16),
        in_specs=vmem_specs(len(parts)),
        out_specs=pl.BlockSpec(memory_space=pltpu.VMEM),
        compiler_params=params(),
        name=name,
    )(*parts)


def add_core_kernel(nout, keep, wkeep, got, *outs):
    rows = keep.shape[0] // nout
    wsum = wkeep[...] + got[pl.ds(rows * nout, BLK)].astype(F32)
    outs[nout][...] = wsum
    for i in range(nout):
        total = keep[pl.ds(i * rows, rows)] + got[pl.ds(i * rows, rows)].astype(F32)
        outs[i][pl.ds(0, rows)] = total.astype(outs[i].dtype)
        if i:
            outs[i][pl.ds(rows, BLK)] = wsum.astype(outs[i].dtype)


def add_core(keep, wkeep, got):
    rows = keep.shape[0] // NY
    return pl.pallas_call(
        functools.partial(add_core_kernel, NY),
        out_shape=[jax.ShapeDtypeStruct((rows, BLK), F32)]
        + [jax.ShapeDtypeStruct((rows + BLK, BLK), BF16)] * (NY - 1)
        + [jax.ShapeDtypeStruct((BLK, BLK), F32)],
        in_specs=vmem_specs(3),
        out_specs=vmem_specs(NY + 1),
        compiler_params=params(),
        name="add_core",
    )(keep, wkeep, got)


def finish_kernel(scale, weight_ref, own, wown, *refs):
    parts, (out_ref, wout_ref) = refs[:-2], refs[-2:]
    rows = own.shape[0]
    total, wsum = own[...], wown[...]
    for part in parts:
        total += part[pl.ds(0, rows)].astype(F32)
        wsum += part[pl.ds(rows, BLK)].astype(F32)
    out_ref[...] = lax.dot_general(
        total.astype(BF16), weight_ref[...], (((1,), (1,)), ((), ())), preferred_element_type=F32
    ).astype(BF16)
    wout_ref[...] = wsum.T * scale


def finish(scale, weight, own, wown, parts):
    return pl.pallas_call(
        functools.partial(finish_kernel, scale),
        out_shape=[
            jax.ShapeDtypeStruct(own.shape, BF16),
            jax.ShapeDtypeStruct((BLK, BLK), F32),
        ],
        in_specs=vmem_specs(3 + len(parts)),
        out_specs=vmem_specs(2),
        compiler_params=params(),
        name="finish",
    )(weight, own, wown, *parts)


def shift_x(a, d):
    return lax.ppermute(a, "col", [(i, (i // NZ + d) % NX * NZ + i % NZ) for i in range(NX * NZ)])


def shift_z(a, d):
    return lax.ppermute(a, "col", [(i, i // NZ * NZ + (i % NZ + d) % NZ) for i in range(NX * NZ)])


def shift_y(a, d):
    return lax.ppermute(a, "row", [(i, (i // 2 + d) % NY * 2 + i % 2) for i in range(NY * 2)])


def swap_core(a):
    return lax.ppermute(a, "row", [(i, i ^ 1) for i in range(NY * 2)])


def local(features, weight, adjacency, row_index, col_index, block_count, grad_out):
    own_rows = features.shape[0]

    beside = [shift_y(features, d) for d in range(1, NY)]
    blocks, codes = prepare(adjacency[0, 0], row_index[0], col_index[0], block_count)
    beside, blocks, codes = lax.optimization_barrier((beside, blocks, codes))
    mine = [features] + beside
    theirs = [swap_core(a) for a in mine]

    feats, x1, x3 = sparse_call(
        functools.partial(forward_odd_kernel, 2 * NY),
        codes,
        blocks,
        mine + theirs,
        [((COL_BLOCKS, BLK, BLK), BF16)] + [((NZ * own_rows, BLK), BF16)] * 2,
        [(HALF + 1, F32)],
        0.5,
        "forward_odd",
    )
    x1, x3 = shift_x(x1, 1), shift_x(x3, 3)
    across, z1, z2, z3 = sparse_call(
        functools.partial(forward_even_kernel, TWO_F),
        codes,
        blocks,
        [feats],
        [((own_rows, BLK), F32)] + [((own_rows, BLK), BF16)] * 3,
        [(HALF // 2 + 1, F32)],
        0.25,
        "forward_two",
    )
    z1, z2, z3 = shift_z(z1, 1), shift_z(z2, 2), shift_z(z3, 3)
    column = sparse_call(
        functools.partial(forward_even_kernel, ZERO_F),
        codes,
        blocks,
        [feats],
        [((NZ * own_rows, BLK), F32)],
        [(HALF // 2 + 1, F32)],
        0.25,
        "forward_zero",
    )[0]
    from_z = [z1, z2, z3]
    own, z1, z2, z3 = add_split([column, x1, x3], [F32, BF16, BF16, BF16], "add_x")
    across, own = lax.optimization_barrier((across, own))
    across = add_split([across] + from_z, [BF16], "add_z")[0]
    parts = [own, shift_z(z1, 1), shift_z(z2, 2), shift_z(z3, 3), shift_x(across, 2)]
    activated, pay = activate(weight, grad_out, parts)

    beside = [shift_z(pay, d) for d in range(1, NZ)]
    across = shift_x(pay, 2)
    column = merge([pay] + beside, "merge_z")
    first, second = shift_x(column, 1), shift_x(column, 3)
    across = [across] + [shift_z(across, d) for d in range(1, NZ)]

    half_rows = COL_BLOCKS // 2 * BLK
    part = sparse_call(
        backward_zero_kernel,
        codes,
        blocks,
        [column],
        [((COL_BLOCKS + 1, BLK, BLK), F32)],
        [(HALF // 2, BF16)],
        0.25,
        "backward_zero",
    )[0]
    part, wpart = sparse_call(
        functools.partial(backward_two_kernel, NZ),
        codes,
        blocks,
        [part, column] + across,
        [((COL_BLOCKS + 1, BLK, BLK), F32), ((BLK, BLK), F32)],
        [(HALF // 2, BF16)],
        0.25,
        "backward_two",
    )
    odd_scratch = [(HALF, BF16), (COL_BLOCKS // 2 + 1, F32)]
    send, wkeep = sparse_call(
        backward_other_kernel,
        codes,
        blocks,
        [part, wpart, first, second],
        [((half_rows + BLK, BLK), F32), ((BLK, BLK), F32)],
        odd_scratch,
        0.25,
        "backward_other",
    )
    got = swap_core(send)
    keep = sparse_call(
        backward_own_kernel,
        codes,
        blocks,
        [part, first, second],
        [((half_rows, BLK), F32)],
        odd_scratch,
        0.25,
        "backward_own",
    )[0]
    parts = add_core(keep, wkeep, got)
    got = [shift_y(parts[d], d) for d in range(1, NY)]
    nodes_all = own_rows * lax.axis_size("row") * lax.axis_size("col")
    input_grad, weight_grad = finish(nodes_all ** (-0.5), weight, parts[0], parts[NY], got)
    return (activated, input_grad, weight_grad)


def solution(mesh):
    placed = (
        P(("col", "row"), None),
        P(),
        P("row", "col", None, None, None),
        P("row", "col", None),
        P("row", "col", None),
        P("row", "col"),
        P(("row", "col"), None),
    )
    return jax.shard_map(
        local,
        mesh=mesh,
        in_specs=placed,
        out_specs=(P(("row", "col"), None), P(("col", "row"), None), P()),
        check_vma=False,
    )
```

```python
import functools

import jax
import jax.numpy as jnp
from jax import lax
from jax.experimental import pallas as pl
from jax.experimental.pallas import tpu as pltpu
from jax.sharding import PartitionSpec as P

BLK = 128
NX = 4
NZ = 4
NY = 4
ROW_BLOCKS = 64
COL_BLOCKS = 32
HALF = 32
OWN = 4
F32 = jnp.float32
BF16 = jnp.bfloat16
VMEM_LIMIT = 24 * 1024 * 1024


def vmem_specs(n):
    return [pl.BlockSpec(memory_space=pltpu.VMEM)] * n


def params():
    return pltpu.CompilerParams(vmem_limit_bytes=VMEM_LIMIT)


ODD_F, TWO_F, ZERO_F, ZERO_B, TWO_B, OTHER_B, OWN_B = range(7)
LISTS = 7
OTHER = NY * OWN


def prepare_kernel(packed_ref, adj_ref, blocks_ref, *refs):
    codes_refs, sem = refs[:-1], refs[-1]
    copy = pltpu.make_async_copy(adj_ref, blocks_ref, sem)
    copy.start()
    row, col = lax.axis_index("row"), lax.axis_index("col")
    y, core = row >> 1, row & 1
    x, z = col >> 2, col & 3
    packed = packed_ref[...]
    alive = packed >= 0
    brow, bcol = packed & (ROW_BLOCKS - 1), packed >> 6
    capacity = packed.shape[1]
    slot = lax.broadcasted_iota(jnp.int32, (1, capacity), 1)
    rx, rz, rb = (brow >> 4) & 3, (brow >> 2) & 3, brow & 3
    cy, cc, cb = (bcol >> 3) & 3, (bcol >> 2) & 1, bcol & 3
    ahead, behind, up = (rx - x) & 3, (x - rx) & 3, (cy - y) & 3
    other = cc ^ core
    odd = ahead & 1
    to_row = odd * (ahead >> 1) * 16 + ((rz - z) & 3) * OWN + rb
    from_row = odd * (behind >> 1) * 16 + ((z - rz) & 3) * OWN + rb
    from_col = other * 16 + ((y - cy) & 3) * OWN + cb
    even = 1 - odd
    to_col = jnp.where(other == 1, 0, even * OTHER) + up * OWN + cb
    kind = jnp.where(odd == 1, 3 - other, ahead >> 1)
    kind = jnp.where(alive, kind, 4)
    row_codes = [
        (slot + 512 * to_row + 65536 * from_col).astype(F32),
        (slot + 512 * to_col + 65536 * from_row).astype(F32),
        kind.astype(F32),
    ]
    member = [(kind == k).astype(F32) for k in range(4)]
    counts = [jnp.sum(m, axis=1, keepdims=True) for m in member]
    lists = [jnp.zeros((1, capacity), F32) for _ in range(LISTS)]
    step = 64
    lane = lax.broadcasted_iota(jnp.int32, (step, capacity), 1)
    place = lane.astype(F32)
    for c in range(0, capacity, step):
        sub = lax.broadcasted_iota(jnp.int32, (step, capacity), 0) + c
        fcode, bcode, ckind = (
            jnp.sum(jnp.where(lane == sub, v, 0.0), axis=1, keepdims=True) for v in row_codes
        )
        ranks = [
            jnp.sum(jnp.where(lane <= sub, m, 0.0), axis=1, keepdims=True) - 1.0 for m in member
        ]
        whole = jnp.where((ckind >= 2.0) & (ckind <= 3.0), ranks[2] + ranks[3] + 1.0, -1.0)
        ranks = [jnp.where(ckind == float(k), r, -1.0) for k, r in enumerate(ranks)]
        for q, rank, code in (
            (ODD_F, whole, fcode),
            (TWO_F, ranks[1], fcode),
            (ZERO_F, ranks[0], fcode),
            (ZERO_B, ranks[0], bcode),
            (TWO_B, ranks[1], bcode),
            (OTHER_B, ranks[2], bcode),
            (OWN_B, ranks[3], bcode),
        ):
            lists[q] += jnp.sum(jnp.where(place == rank, code, 0.0), axis=0, keepdims=True)
    where = slot.astype(F32)
    for q, count, idle in (
        (ODD_F, counts[2] + counts[3], HALF),
        (TWO_F, counts[1], HALF // 2),
        (ZERO_F, counts[0], HALF // 2),
        (ZERO_B, counts[0], COL_BLOCKS),
        (TWO_B, counts[1], COL_BLOCKS),
        (OTHER_B, counts[2], OTHER),
        (OWN_B, counts[3], OTHER),
    ):
        codes_refs[q][:, 0:capacity] = jnp.where(where < count, lists[q], 512.0 * idle).astype(jnp.int32)
        codes_refs[q][:, capacity : capacity + BLK] = jnp.broadcast_to(count, (1, BLK)).astype(jnp.int32)
    copy.wait()


def prepare(adjacency, packed):
    capacity = adjacency.shape[0]
    return pl.pallas_call(
        prepare_kernel,
        out_shape=[
            jax.ShapeDtypeStruct(adjacency.shape, adjacency.dtype),
        ]
        + [jax.ShapeDtypeStruct((1, capacity + BLK), jnp.int32)] * LISTS,
        in_specs=vmem_specs(1) + [pl.BlockSpec(memory_space=pl.ANY)],
        out_specs=vmem_specs(1 + LISTS),
        scratch_shapes=[pltpu.SemaphoreType.DMA],
        compiler_params=params(),
        cost_estimate=pl.CostEstimate(flops=0, bytes_accessed=2 * adjacency.size * 2, transcendentals=0),
        name="prepare",
    )(packed, adjacency)


def accumulate(unroll, codes_ref, acc, product):
    @pl.loop(0, pl.cdiv(codes_ref[0, codes_ref.shape[1] - BLK], unroll))
    def _(g):
        codes = [codes_ref[0, g * unroll + j] for j in range(unroll)]
        prods = [product(c & 511, c >> 16) for c in codes]
        for j in range(unroll):
            acc[(codes[j] >> 9) & 127] += prods[j]


def sparse_cost(share):
    return pl.CostEstimate(
        flops=int(512 * BLK**3 * 8 * share), bytes_accessed=int(20 * 2**20 * share), transcendentals=0
    )


def sparse_call(kernel, codes, adjacency, operands, outs, scratch, share, name):
    return pl.pallas_call(
        kernel,
        out_shape=[jax.ShapeDtypeStruct(shape, dtype) for shape, dtype in outs],
        in_specs=[pl.BlockSpec(memory_space=pltpu.SMEM)] + vmem_specs(1 + len(operands)),
        out_specs=vmem_specs(len(outs)),
        scratch_shapes=[pltpu.VMEM((blocks, BLK, BLK), dtype) for blocks, dtype in scratch],
        compiler_params=params(),
        cost_estimate=sparse_cost(share),
        name=name,
    )(codes, adjacency, *operands)


def write_rows(acc, outs):
    at = 0
    for out in outs:
        blocks = out.shape[0] // BLK
        out[...] = acc[pl.ds(at, blocks)].reshape(out.shape).astype(out.dtype)
        at += blocks


def forward_odd_kernel(nin, codes_ref, adj_ref, *refs):
    ins, (feats, *outs), acc = refs[:nin], refs[nin:-1], refs[-1]
    per = feats.shape[0] // nin
    for i in range(nin):
        feats[pl.ds(i * per, per)] = ins[i][...].reshape(per, BLK, BLK)
    acc[...] = jnp.zeros_like(acc)

    def product(slot, source):
        return jnp.dot(adj_ref[slot], feats[source], preferred_element_type=F32)

    accumulate(64, codes_ref, acc, product)
    write_rows(acc, outs)


def forward_even_kernel(codes_ref, adj_ref, feats, *refs):
    outs, acc = refs[:-1], refs[-1]
    acc[...] = jnp.zeros_like(acc)

    def product(slot, source):
        return jnp.dot(adj_ref[slot], feats[source], preferred_element_type=F32)

    accumulate(32, codes_ref, acc, product)
    write_rows(acc, outs)


def gather_slopes(slopes, ins):
    at = 0
    for part in ins:
        blocks = part.shape[0] // BLK - 1
        slopes[pl.ds(at, blocks)] = part[pl.ds(0, blocks * BLK)].reshape(blocks, BLK, BLK)
        at += blocks


def last_block(part):
    return part[pl.ds(part.shape[0] - BLK, BLK)].astype(F32)


def backward_zero_kernel(codes_ref, adj_ref, column, acc, slopes):
    gather_slopes(slopes, [column])
    acc[...] = jnp.zeros_like(acc)

    def product(slot, source):
        return jnp.dot(slopes[source], adj_ref[slot], preferred_element_type=F32)

    accumulate(32, codes_ref, acc, product)


def backward_two_kernel(nin, codes_ref, adj_ref, before, column, *refs):
    ins, (acc, wsum), slopes = refs[:nin], refs[nin : nin + 2], refs[-1]
    gather_slopes(slopes, ins)
    acc[...] = before[...]

    def product(slot, source):
        return jnp.dot(slopes[source], adj_ref[slot], preferred_element_type=F32)

    accumulate(32, codes_ref, acc, product)
    wsum[...] = last_block(column) + sum(last_block(part) for part in ins)


def backward_other_kernel(codes_ref, adj_ref, before, wpart, first, second, send, wsum, slopes, acc):
    gather_slopes(slopes, [first, second])
    acc[...] = before[pl.ds(0, OTHER + 1)]

    def product(slot, source):
        return jnp.dot(slopes[source], adj_ref[slot], preferred_element_type=F32)

    accumulate(32, codes_ref, acc, product)
    for b in range(OTHER):
        send[pl.ds(b * BLK, BLK)] = acc[b].T
    total = wpart[...] + last_block(first) + last_block(second)
    wsum[...] = total
    send[pl.ds(OTHER * BLK, BLK)] = total


def backward_own_kernel(unroll, start, codes_ref, adj_ref, before, slopes, keep, acc):
    blocks = acc.shape[0] - 1
    acc[...] = before[pl.ds(start, blocks + 1)]

    def product(slot, source):
        return jnp.dot(slopes[source], adj_ref[slot], preferred_element_type=F32)

    accumulate(unroll, codes_ref, acc, product)
    for b in range(blocks):
        keep[pl.ds(b * BLK, BLK)] = acc[b].T


def add_split_kernel(nin, *refs):
    ins, outs = refs[:nin], refs[nin:]
    at = 0
    for out in outs:
        rows = out.shape[0]
        total = ins[0][pl.ds(at, rows)].astype(F32)
        for part in ins[1:]:
            total += part[pl.ds(at, rows)].astype(F32)
        out[...] = total.astype(out.dtype)
        at += rows


def add_split(parts, dtypes, name):
    rows = parts[0].shape[0] // len(dtypes)
    return pl.pallas_call(
        functools.partial(add_split_kernel, len(parts)),
        out_shape=[jax.ShapeDtypeStruct((rows, BLK), dtype) for dtype in dtypes],
        in_specs=vmem_specs(len(parts)),
        out_specs=vmem_specs(len(dtypes)),
        compiler_params=params(),
        name=name,
    )(*parts)


def activate_kernel(weight_ref, grad_ref, *refs):
    parts, (act_ref, pay_ref) = refs[:-2], refs[-2:]
    rows = act_ref.shape[0]
    total = parts[0][...]
    for part in parts[1:]:
        total += part[...].astype(F32)
    high = total.astype(BF16)
    rest = total - high.astype(F32)
    low = rest.astype(BF16)
    lowest = (rest - low.astype(F32)).astype(BF16)
    weight = weight_ref[...]
    pre = jnp.dot(lowest, weight, preferred_element_type=F32)
    pre += jnp.dot(low, weight, preferred_element_type=F32)
    pre += jnp.dot(high, weight, preferred_element_type=F32)
    squash = jnp.tanh(pre)
    act_ref[...] = squash.astype(BF16)
    slope = (grad_ref[...].astype(F32) * (1.0 - squash * squash)).astype(BF16)
    wterm = jnp.zeros((BLK, BLK), F32)
    for b in range(0, rows, BLK):
        turned = slope[b : b + BLK].T
        pay_ref[pl.ds(b, BLK)] = turned
        wterm += jnp.dot(turned, high[b : b + BLK], preferred_element_type=F32)
        wterm += jnp.dot(turned, low[b : b + BLK], preferred_element_type=F32)
    pay_ref[pl.ds(rows, BLK)] = wterm.astype(BF16)


def activate(weight, grad_out, parts):
    rows = grad_out.shape[0]
    return pl.pallas_call(
        activate_kernel,
        out_shape=[
            jax.ShapeDtypeStruct((rows, BLK), BF16),
            jax.ShapeDtypeStruct((rows + BLK, BLK), BF16),
        ],
        in_specs=vmem_specs(2 + len(parts)),
        out_specs=vmem_specs(2),
        compiler_params=params(),
        name="activate",
    )(weight, grad_out, *parts)


def merge_kernel(*refs):
    parts, out = refs[:-1], refs[-1]
    rows = parts[0].shape[0] - BLK
    total = jnp.zeros((BLK, BLK), F32)
    for i, part in enumerate(parts):
        out[pl.ds(i * rows, rows)] = part[pl.ds(0, rows)]
        total += last_block(part)
    out[pl.ds(len(parts) * rows, BLK)] = total.astype(BF16)


def merge(parts, name):
    rows = len(parts) * (parts[0].shape[0] - BLK) + BLK
    return pl.pallas_call(
        merge_kernel,
        out_shape=jax.ShapeDtypeStruct((rows, BLK), BF16),
        in_specs=vmem_specs(len(parts)),
        out_specs=pl.BlockSpec(memory_space=pltpu.VMEM),
        compiler_params=params(),
        name=name,
    )(*parts)


def add_core_kernel(keep, wkeep, got, *outs):
    parts, own, wown = outs[:-2], outs[-2], outs[-1]
    rows = own.shape[0]
    wsum = wkeep[...] + last_block(got)
    wown[...] = wsum
    own[...] = keep[pl.ds(0, rows)] + got[pl.ds(0, rows)]
    for i, part in enumerate(parts, 1):
        part[pl.ds(0, rows)] = (keep[pl.ds(i * rows, rows)] + got[pl.ds(i * rows, rows)]).astype(BF16)
        part[pl.ds(rows, BLK)] = wsum.astype(BF16)


def add_core(keep, wkeep, got):
    rows = keep.shape[0] // NY
    return pl.pallas_call(
        add_core_kernel,
        out_shape=[jax.ShapeDtypeStruct((rows + BLK, BLK), BF16)] * (NY - 1)
        + [jax.ShapeDtypeStruct((rows, BLK), F32), jax.ShapeDtypeStruct((BLK, BLK), F32)],
        in_specs=vmem_specs(3),
        out_specs=vmem_specs(NY + 1),
        compiler_params=params(),
        name="add_core",
    )(keep, wkeep, got)


def finish_kernel(scale, weight_ref, own, wown, *refs):
    parts, (out_ref, wout_ref) = refs[:-2], refs[-2:]
    rows = own.shape[0]
    total, wsum = own[...], wown[...]
    for part in parts:
        total += part[pl.ds(0, rows)].astype(F32)
        wsum += part[pl.ds(rows, BLK)].astype(F32)
    out_ref[...] = lax.dot_general(
        total.astype(BF16), weight_ref[...], (((1,), (1,)), ((), ())), preferred_element_type=F32
    ).astype(BF16)
    wout_ref[...] = wsum.T * scale


def finish(scale, weight, own, wown, parts):
    return pl.pallas_call(
        functools.partial(finish_kernel, scale),
        out_shape=[
            jax.ShapeDtypeStruct(own.shape, BF16),
            jax.ShapeDtypeStruct((BLK, BLK), F32),
        ],
        in_specs=vmem_specs(3 + len(parts)),
        out_specs=vmem_specs(2),
        compiler_params=params(),
        name="finish",
    )(weight, own, wown, *parts)


def shift_x(a, d):
    return lax.ppermute(a, "col", [(i, (i // NZ + d) % NX * NZ + i % NZ) for i in range(NX * NZ)])


def shift_z(a, d):
    return lax.ppermute(a, "col", [(i, i // NZ * NZ + (i % NZ + d) % NZ) for i in range(NX * NZ)])


def shift_y(a, d):
    return lax.ppermute(a, "row", [(i, (i // 2 + d) % NY * 2 + i % 2) for i in range(NY * 2)])


def swap_core(a):
    return lax.ppermute(a, "row", [(i, i ^ 1) for i in range(NY * 2)])


def local(features, weight, adjacency, row_index, col_index, block_count, grad_out):
    own_rows = features.shape[0]

    beside = [shift_y(features, d) for d in range(1, NY)]
    alive = jnp.arange(adjacency.shape[2], dtype=jnp.int32)[None] < block_count
    packed = jnp.where(alive, row_index[0] + ROW_BLOCKS * col_index[0], -1)
    blocks, *codes = prepare(adjacency[0, 0], packed)
    beside, blocks, codes = lax.optimization_barrier((beside, blocks, codes))
    mine = [features] + beside
    theirs = [swap_core(a) for a in mine]

    feats, x1, x3 = sparse_call(
        functools.partial(forward_odd_kernel, 2 * NY),
        codes[ODD_F],
        blocks,
        mine + theirs,
        [((COL_BLOCKS, BLK, BLK), BF16)] + [((NZ * own_rows, BLK), BF16)] * 2,
        [(HALF + 1, F32)],
        0.5,
        "forward_odd",
    )
    x1, x3 = shift_x(x1, 1), shift_x(x3, 3)
    across, z1, z2, z3 = sparse_call(
        forward_even_kernel,
        codes[TWO_F],
        blocks,
        [feats],
        [((own_rows, BLK), F32)] + [((own_rows, BLK), BF16)] * 3,
        [(HALF // 2 + 1, F32)],
        0.25,
        "forward_two",
    )
    z1, z2, z3 = shift_z(z1, 1), shift_z(z2, 2), shift_z(z3, 3)
    column = sparse_call(
        forward_even_kernel,
        codes[ZERO_F],
        blocks,
        [feats],
        [((NZ * own_rows, BLK), F32)],
        [(HALF // 2 + 1, F32)],
        0.25,
        "forward_zero",
    )[0]
    from_z = [z1, z2, z3]
    own, z1, z2, z3 = add_split([column, x1, x3], [F32, BF16, BF16, BF16], "add_x")
    across, own = lax.optimization_barrier((across, own))
    across = add_split([across] + from_z, [BF16], "add_z")[0]
    parts = [own, shift_z(z1, 1), shift_z(z2, 2), shift_z(z3, 3), shift_x(across, 2)]
    activated, pay = activate(weight, grad_out, parts)

    beside = [shift_z(pay, d) for d in range(1, NZ)]
    across = shift_x(pay, 2)
    column = merge([pay] + beside, "merge_z")
    first, second = shift_x(column, 1), shift_x(column, 3)
    across = [across] + [shift_z(across, d) for d in range(1, NZ)]

    part = sparse_call(
        backward_zero_kernel,
        codes[ZERO_B],
        blocks,
        [column],
        [((COL_BLOCKS + 1, BLK, BLK), F32)],
        [(HALF // 2, BF16)],
        0.25,
        "backward_zero",
    )[0]
    part, wpart = sparse_call(
        functools.partial(backward_two_kernel, NZ),
        codes[TWO_B],
        blocks,
        [part, column] + across,
        [((COL_BLOCKS + 1, BLK, BLK), F32), ((BLK, BLK), F32)],
        [(HALF // 2, BF16)],
        0.25,
        "backward_two",
    )
    send, wkeep, slopes = sparse_call(
        backward_other_kernel,
        codes[OTHER_B],
        blocks,
        [part, wpart, first, second],
        [(((OTHER + 1) * BLK, BLK), F32), ((BLK, BLK), F32), ((HALF, BLK, BLK), BF16)],
        [(OTHER + 1, F32)],
        0.25,
        "backward_other",
    )
    got = swap_core(send)
    keep = sparse_call(
        functools.partial(backward_own_kernel, 32, OTHER),
        codes[OWN_B],
        blocks,
        [part, slopes],
        [((OTHER * BLK, BLK), F32)],
        [(OTHER + 1, F32)],
        0.25,
        "backward_own",
    )[0]
    *parts, own, wown = add_core(keep, wkeep, got)
    parts = [shift_y(part, d) for d, part in enumerate(parts, 1)]
    nodes_all = own_rows * lax.axis_size("row") * lax.axis_size("col")
    input_grad, weight_grad = finish(nodes_all ** (-0.5), weight, own, wown, parts)
    return (activated, input_grad, weight_grad)


def solution(mesh):
    placed = (
        P(("col", "row"), None),
        P(),
        P("row", "col", None, None, None),
        P("row", "col", None),
        P("row", "col", None),
        P("row", "col"),
        P(("row", "col"), None),
    )
    return jax.shard_map(
        local,
        mesh=mesh,
        in_specs=placed,
        out_specs=(P(("row", "col"), None), P(("col", "row"), None), P()),
        check_vma=False,
    )
```

```python
import functools

import jax
import jax.numpy as jnp
from jax import lax
from jax.experimental import pallas as pl
from jax.experimental.pallas import tpu as pltpu
from jax.sharding import PartitionSpec as P

BLK = 128
NX = 4
NZ = 4
NY = 4
ROW_BLOCKS = 64
COL_BLOCKS = 32
OWN = 4
F32 = jnp.float32
BF16 = jnp.bfloat16
VMEM_LIMIT = 24 * 1024 * 1024


def vmem_specs(n):
    return [pl.BlockSpec(memory_space=pltpu.VMEM)] * n


def params():
    return pltpu.CompilerParams(vmem_limit_bytes=VMEM_LIMIT)


FAR_F, TWO_F, REST_F, EARLY_B, OTHER_B, OWN_B = range(6)
LISTS = 6
FAR = (NZ - 1) * OWN
OTHER = NY * OWN


def prepare_kernel(packed_ref, adj_ref, blocks_ref, *refs):
    codes_refs, sem = refs[:-1], refs[-1]
    copy = pltpu.make_async_copy(adj_ref, blocks_ref, sem)
    copy.start()
    row, col = lax.axis_index("row"), lax.axis_index("col")
    y, core = row >> 1, row & 1
    x, z = col >> 2, col & 3
    packed = packed_ref[...]
    alive = packed >= 0
    brow, bcol = packed & (ROW_BLOCKS - 1), packed >> 6
    capacity = packed.shape[1]
    slot = lax.broadcasted_iota(jnp.int32, (1, capacity), 1)
    rx, rz, rb = (brow >> 4) & 3, (brow >> 2) & 3, brow & 3
    cy, cc, cb = (bcol >> 3) & 3, (bcol >> 2) & 1, bcol & 3
    ahead, behind, up = (rx - x) & 3, (x - rx) & 3, (cy - y) & 3
    ahead_z, behind_z = (rz - z) & 3, (z - rz) & 3
    other = cc ^ core
    odd, level = ahead & 1, ahead_z == 0
    far = (odd == 1) & (ahead_z > 0)
    rest = (ahead == 0) | ((odd == 1) & level)
    near_row = jnp.where(odd == 1, NZ * OWN + (ahead >> 1) * OWN + rb, ahead_z * OWN + rb)
    to_row = jnp.where(far, (ahead >> 1) * FAR + (ahead_z - 1) * OWN + rb, near_row)
    near_row = jnp.where(odd == 1, NZ * OWN + (behind >> 1) * OWN + rb, behind_z * OWN + rb)
    near_row = jnp.where((ahead == 2) & level, (NZ + 2) * OWN + rb, near_row)
    near_row = jnp.where((ahead == 2) & (ahead_z > 0), near_row - OWN, near_row)
    from_row = jnp.where(far, FAR + (behind >> 1) * FAR + (behind_z - 1) * OWN + rb, near_row)
    to_col = jnp.where((rest | ((ahead == 2) & level)) & (other == 0), OTHER, 0) + up * OWN + cb
    from_col = other * 16 + ((y - cy) & 3) * OWN + cb
    forward_kind = jnp.where(rest, 2, jnp.where(far, 0, 1))
    forward_kind = jnp.where(alive, forward_kind, 3)
    early = rest | ((ahead == 2) & level)
    backward_kind = jnp.where(early, 2, 1 - other)
    backward_kind = jnp.where(alive, backward_kind, 3)
    row_codes = [
        (slot + 512 * to_row + 65536 * from_col).astype(F32),
        (slot + 512 * to_col + 65536 * from_row).astype(F32),
        forward_kind.astype(F32),
        backward_kind.astype(F32),
    ]
    member = [(forward_kind == k).astype(F32) for k in range(3)] + [(backward_kind == k).astype(F32) for k in range(3)]
    counts = [jnp.sum(m, axis=1, keepdims=True) for m in member]
    lists = [jnp.zeros((1, capacity), F32) for _ in range(LISTS)]
    step = 64
    lane = lax.broadcasted_iota(jnp.int32, (step, capacity), 1)
    place = lane.astype(F32)
    for c in range(0, capacity, step):
        sub = lax.broadcasted_iota(jnp.int32, (step, capacity), 0) + c
        fcode, bcode, fkind, bkind = (
            jnp.sum(jnp.where(lane == sub, v, 0.0), axis=1, keepdims=True) for v in row_codes
        )
        ranks = [
            jnp.sum(jnp.where(lane <= sub, m, 0.0), axis=1, keepdims=True) - 1.0 for m in member
        ]
        kinds = [(fkind, 0.0), (fkind, 1.0), (fkind, 2.0), (bkind, 0.0), (bkind, 1.0), (bkind, 2.0)]
        ranks = [jnp.where(kind == k, r, -1.0) for (kind, k), r in zip(kinds, ranks)]
        for q, rank, code in (
            (FAR_F, ranks[0], fcode),
            (TWO_F, ranks[1], fcode),
            (REST_F, ranks[2], fcode),
            (EARLY_B, ranks[5], bcode),
            (OTHER_B, ranks[3], bcode),
            (OWN_B, ranks[4], bcode),
        ):
            lists[q] += jnp.sum(jnp.where(place == rank, code, 0.0), axis=0, keepdims=True)
    where = slot.astype(F32)
    for q, count, idle in (
        (FAR_F, counts[0], 2 * FAR),
        (TWO_F, counts[1], NZ * OWN),
        (REST_F, counts[2], (NZ + 2) * OWN),
        (EARLY_B, counts[5], COL_BLOCKS),
        (OTHER_B, counts[3], OTHER),
        (OWN_B, counts[4], OTHER),
    ):
        codes_refs[q][:, 0:capacity] = jnp.where(where < count, lists[q], 512.0 * idle).astype(jnp.int32)
        codes_refs[q][:, capacity : capacity + BLK] = jnp.broadcast_to(count, (1, BLK)).astype(jnp.int32)
    copy.wait()


def prepare(adjacency, packed):
    capacity = adjacency.shape[0]
    return pl.pallas_call(
        prepare_kernel,
        out_shape=[
            jax.ShapeDtypeStruct(adjacency.shape, adjacency.dtype),
        ]
        + [jax.ShapeDtypeStruct((1, capacity + BLK), jnp.int32)] * LISTS,
        in_specs=vmem_specs(1) + [pl.BlockSpec(memory_space=pl.ANY)],
        out_specs=vmem_specs(1 + LISTS),
        scratch_shapes=[pltpu.SemaphoreType.DMA],
        compiler_params=params(),
        cost_estimate=pl.CostEstimate(flops=0, bytes_accessed=2 * adjacency.size * 2, transcendentals=0),
        name="prepare",
    )(packed, adjacency)


def accumulate(unroll, codes_ref, acc, product):
    @pl.loop(0, pl.cdiv(codes_ref[0, codes_ref.shape[1] - BLK], unroll))
    def _(g):
        codes = [codes_ref[0, g * unroll + j] for j in range(unroll)]
        prods = [product(c & 511, c >> 16) for c in codes]
        for j in range(unroll):
            acc[(codes[j] >> 9) & 127] += prods[j]


def sparse_cost(share):
    return pl.CostEstimate(
        flops=int(512 * BLK**3 * 8 * share), bytes_accessed=int(20 * 2**20 * share), transcendentals=0
    )


def sparse_call(kernel, codes, adjacency, operands, outs, scratch, share, name):
    return pl.pallas_call(
        kernel,
        out_shape=[jax.ShapeDtypeStruct(shape, dtype) for shape, dtype in outs],
        in_specs=[pl.BlockSpec(memory_space=pltpu.SMEM)] + vmem_specs(1 + len(operands)),
        out_specs=vmem_specs(len(outs)),
        scratch_shapes=[pltpu.VMEM((blocks, BLK, BLK), dtype) for blocks, dtype in scratch],
        compiler_params=params(),
        cost_estimate=sparse_cost(share),
        name=name,
    )(codes, adjacency, *operands)


def write_rows(acc, outs):
    at = 0
    for out in outs:
        blocks = out.shape[0] // BLK
        out[...] = acc[pl.ds(at, blocks)].reshape(out.shape).astype(out.dtype)
        at += blocks


def forward_far_kernel(nin, codes_ref, adj_ref, *refs):
    ins, (feats, *outs), acc = refs[:nin], refs[nin:-1], refs[-1]
    per = feats.shape[0] // nin
    for i in range(nin):
        feats[pl.ds(i * per, per)] = ins[i][...].reshape(per, BLK, BLK)
    acc[...] = jnp.zeros_like(acc)

    def product(slot, source):
        return jnp.dot(adj_ref[slot], feats[source], preferred_element_type=F32)

    accumulate(64, codes_ref, acc, product)
    write_rows(acc, outs)


def forward_near_kernel(unroll, codes_ref, adj_ref, feats, *refs):
    outs, acc = refs[:-1], refs[-1]
    acc[...] = jnp.zeros_like(acc)

    def product(slot, source):
        return jnp.dot(adj_ref[slot], feats[source], preferred_element_type=F32)

    accumulate(unroll, codes_ref, acc, product)
    write_rows(acc, outs)


def gather_slopes(slopes, ins):
    at = 0
    for part in ins:
        blocks = part.shape[0] // BLK - 1
        slopes[pl.ds(at, blocks)] = part[pl.ds(0, blocks * BLK)].reshape(blocks, BLK, BLK)
        at += blocks


def last_block(part):
    return part[pl.ds(part.shape[0] - BLK, BLK)].astype(F32)


def backward_early_kernel(nin, codes_ref, adj_ref, *refs):
    ins, acc, slopes = refs[:nin], refs[nin], refs[nin + 1]
    gather_slopes(slopes, ins)
    acc[...] = jnp.zeros_like(acc)

    def product(slot, source):
        return jnp.dot(slopes[source], adj_ref[slot], preferred_element_type=F32)

    accumulate(64, codes_ref, acc, product)


def backward_other_kernel(nin, codes_ref, adj_ref, before, rest, level, *refs):
    ins, (send, wsum, slopes), acc = refs[:nin], refs[nin : nin + 3], refs[-1]
    gather_slopes(slopes, ins)
    acc[...] = before[pl.ds(0, OTHER + 1)]

    def product(slot, source):
        return jnp.dot(slopes[source], adj_ref[slot], preferred_element_type=F32)

    accumulate(64, codes_ref, acc, product)
    send[pl.ds(0, OTHER * BLK)] = acc[pl.ds(0, OTHER)].reshape(OTHER * BLK, BLK)
    total = last_block(rest) + last_block(level) + sum(last_block(part) for part in ins)
    wsum[...] = total
    send[pl.ds(OTHER * BLK, BLK)] = total


def backward_own_kernel(codes_ref, adj_ref, before, slopes, keep, acc):
    acc[...] = before[pl.ds(OTHER, OTHER + 1)]

    def product(slot, source):
        return jnp.dot(slopes[source], adj_ref[slot], preferred_element_type=F32)

    accumulate(64, codes_ref, acc, product)
    keep[...] = acc[pl.ds(0, OTHER)].reshape(keep.shape)


def add_split_kernel(nin, *refs):
    ins, outs = refs[:nin], refs[nin:]
    at = 0
    for out in outs:
        rows = out.shape[0]
        total = ins[0][pl.ds(at, rows)].astype(F32)
        for part in ins[1:]:
            total += part[pl.ds(at, rows)].astype(F32)
        out[...] = total.astype(out.dtype)
        at += rows


def add_split(parts, dtypes, name):
    rows = parts[0].shape[0] // len(dtypes)
    return pl.pallas_call(
        functools.partial(add_split_kernel, len(parts)),
        out_shape=[jax.ShapeDtypeStruct((rows, BLK), dtype) for dtype in dtypes],
        in_specs=vmem_specs(len(parts)),
        out_specs=vmem_specs(len(dtypes)),
        compiler_params=params(),
        name=name,
    )(*parts)


def activate_kernel(weight_ref, grad_ref, *refs):
    parts, (act_ref, pay_ref) = refs[:-2], refs[-2:]
    rows = act_ref.shape[0]
    total = parts[0][...]
    for part in parts[1:]:
        total += part[...].astype(F32)
    high = total.astype(BF16)
    rest = total - high.astype(F32)
    low = rest.astype(BF16)
    lowest = (rest - low.astype(F32)).astype(BF16)
    weight = weight_ref[...]
    pre = jnp.dot(lowest, weight, preferred_element_type=F32)
    pre += jnp.dot(low, weight, preferred_element_type=F32)
    pre += jnp.dot(high, weight, preferred_element_type=F32)
    squash = jnp.tanh(pre)
    act_ref[...] = squash.astype(BF16)
    slope = (grad_ref[...].astype(F32) * (1.0 - squash * squash)).astype(BF16)
    wterm = jnp.zeros((BLK, BLK), F32)
    for b in range(0, rows, BLK):
        turned = slope[b : b + BLK].T
        pay_ref[pl.ds(b, BLK)] = turned
        wterm += jnp.dot(turned, high[b : b + BLK], preferred_element_type=F32)
        wterm += jnp.dot(turned, low[b : b + BLK], preferred_element_type=F32)
    pay_ref[pl.ds(rows, BLK)] = wterm.astype(BF16)


def activate(weight, grad_out, parts):
    rows = grad_out.shape[0]
    return pl.pallas_call(
        activate_kernel,
        out_shape=[
            jax.ShapeDtypeStruct((rows, BLK), BF16),
            jax.ShapeDtypeStruct((rows + BLK, BLK), BF16),
        ],
        in_specs=vmem_specs(2 + len(parts)),
        out_specs=vmem_specs(2),
        compiler_params=params(),
        name="activate",
    )(weight, grad_out, *parts)


def merge_kernel(own, *refs):
    parts, out = refs[:-1], refs[-1]
    rows = own.shape[0] - BLK
    total = last_block(own)
    for i, part in enumerate(parts):
        out[pl.ds(i * rows, rows)] = part[pl.ds(0, rows)]
        total += last_block(part)
    out[pl.ds(len(parts) * rows, BLK)] = total.astype(BF16)


def merge(own, parts):
    rows = len(parts) * (own.shape[0] - BLK) + BLK
    return pl.pallas_call(
        merge_kernel,
        out_shape=jax.ShapeDtypeStruct((rows, BLK), BF16),
        in_specs=vmem_specs(1 + len(parts)),
        out_specs=pl.BlockSpec(memory_space=pltpu.VMEM),
        compiler_params=params(),
        name="merge_z",
    )(own, *parts)


def add_core_kernel(keep, wkeep, got, *outs):
    parts, own, wown = outs[:-2], outs[-2], outs[-1]
    rows = own.shape[0]
    wsum = wkeep[...] + last_block(got)
    wown[...] = wsum
    own[...] = keep[pl.ds(0, rows)] + got[pl.ds(0, rows)]
    for i, part in enumerate(parts, 1):
        part[pl.ds(0, rows)] = (keep[pl.ds(i * rows, rows)] + got[pl.ds(i * rows, rows)]).astype(BF16)
        part[pl.ds(rows, BLK)] = wsum.astype(BF16)


def add_core(keep, wkeep, got):
    rows = keep.shape[0] // NY
    return pl.pallas_call(
        add_core_kernel,
        out_shape=[jax.ShapeDtypeStruct((rows + BLK, BLK), BF16)] * (NY - 1)
        + [jax.ShapeDtypeStruct((rows, BLK), F32), jax.ShapeDtypeStruct((BLK, BLK), F32)],
        in_specs=vmem_specs(3),
        out_specs=vmem_specs(NY + 1),
        compiler_params=params(),
        name="add_core",
    )(keep, wkeep, got)


def finish_kernel(scale, weight_ref, own, wown, *refs):
    parts, (out_ref, wout_ref) = refs[:-2], refs[-2:]
    rows = own.shape[0]
    total, wsum = own[...], wown[...]
    for part in parts:
        total += part[pl.ds(0, rows)].astype(F32)
        wsum += part[pl.ds(rows, BLK)].astype(F32)
    turned = total.astype(BF16)
    for b in range(0, rows, BLK):
        block = jnp.dot(weight_ref[...], turned[b : b + BLK], preferred_element_type=F32)
        out_ref[pl.ds(b, BLK)] = block.T.astype(BF16)
    wout_ref[...] = wsum.T * scale


def finish(scale, weight, own, wown, parts):
    return pl.pallas_call(
        functools.partial(finish_kernel, scale),
        out_shape=[
            jax.ShapeDtypeStruct(own.shape, BF16),
            jax.ShapeDtypeStruct((BLK, BLK), F32),
        ],
        in_specs=vmem_specs(3 + len(parts)),
        out_specs=vmem_specs(2),
        compiler_params=params(),
        name="finish",
    )(weight, own, wown, *parts)


def shift_x(a, d):
    return lax.ppermute(a, "col", [(i, (i // NZ + d) % NX * NZ + i % NZ) for i in range(NX * NZ)])


def shift_z(a, d):
    return lax.ppermute(a, "col", [(i, i // NZ * NZ + (i % NZ + d) % NZ) for i in range(NX * NZ)])


def shift_y(a, d):
    return lax.ppermute(a, "row", [(i, (i // 2 + d) % NY * 2 + i % 2) for i in range(NY * 2)])


def swap_core(a):
    return lax.ppermute(a, "row", [(i, i ^ 1) for i in range(NY * 2)])


def local(features, weight, adjacency, row_index, col_index, block_count, grad_out):
    own_rows = features.shape[0]

    beside = [shift_y(features, d) for d in range(1, NY)]
    alive = jnp.arange(adjacency.shape[2], dtype=jnp.int32)[None] < block_count
    packed = jnp.where(alive, row_index[0] + ROW_BLOCKS * col_index[0], -1)
    blocks, *codes = prepare(adjacency[0, 0], packed)
    beside, blocks, codes = lax.optimization_barrier((beside, blocks, codes))
    mine = [features] + beside
    theirs = [swap_core(a) for a in mine]

    feats, x1, x3 = sparse_call(
        functools.partial(forward_far_kernel, 2 * NY),
        codes[FAR_F],
        blocks,
        mine + theirs,
        [((COL_BLOCKS, BLK, BLK), BF16)] + [((FAR * BLK, BLK), BF16)] * 2,
        [(2 * FAR + 1, F32)],
        0.375,
        "forward_far",
    )
    x1, x3 = shift_x(x1, 1), shift_x(x3, 3)
    across, z1, z2, z3 = sparse_call(
        functools.partial(forward_near_kernel, 32),
        codes[TWO_F],
        blocks,
        [feats],
        [((own_rows, BLK), F32)] + [((own_rows, BLK), BF16)] * 3,
        [(NZ * OWN + 1, F32)],
        0.25,
        "forward_two",
    )
    z1, z2, z3 = shift_z(z1, 1), shift_z(z2, 2), shift_z(z3, 3)
    own, column, n1, n3 = sparse_call(
        functools.partial(forward_near_kernel, 64),
        codes[REST_F],
        blocks,
        [feats],
        [((own_rows, BLK), F32), ((FAR * BLK, BLK), F32)] + [((own_rows, BLK), BF16)] * 2,
        [((NZ + 2) * OWN + 1, F32)],
        0.375,
        "forward_rest",
    )
    from_z = [z1, z2, z3]
    z1, z2, z3 = add_split([column, x1, x3], [BF16] * 3, "add_x")
    across, z1, n1, n3 = lax.optimization_barrier((across, z1, n1, n3))
    z1, z2, z3 = shift_z(z1, 1), shift_z(z2, 2), shift_z(z3, 3)
    across = add_split([across] + from_z, [BF16], "add_z")[0]
    parts = [own, z1, z2, z3, shift_x(n1, 1), shift_x(n3, 3), shift_x(across, 2)]
    activated, pay = activate(weight, grad_out, parts)

    beside = [shift_z(pay, d) for d in range(1, NZ)]
    across = shift_x(pay, 2)
    n1, n3 = shift_x(pay, 1), shift_x(pay, 3)
    rest = merge(pay, beside)
    first, second = shift_x(rest, 1), shift_x(rest, 3)
    across = [across] + [shift_z(across, d) for d in range(1, NZ)]

    part = sparse_call(
        functools.partial(backward_early_kernel, 5),
        codes[EARLY_B],
        blocks,
        [pay, rest, n1, n3, across[0]],
        [((COL_BLOCKS + 1, BLK, BLK), F32)],
        [((NZ + 3) * OWN, BF16)],
        0.375,
        "backward_early",
    )[0]
    late = 3 * FAR
    send, wkeep, slopes = sparse_call(
        functools.partial(backward_other_kernel, NZ + 1),
        codes[OTHER_B],
        blocks,
        [part, rest, across[0]] + across[1:] + [first, second],
        [(((OTHER + 1) * BLK, BLK), F32), ((BLK, BLK), F32), ((late, BLK, BLK), BF16)],
        [(OTHER + 1, F32)],
        0.3,
        "backward_other",
    )
    got = swap_core(send)
    keep = sparse_call(
        backward_own_kernel,
        codes[OWN_B],
        blocks,
        [part, slopes],
        [((OTHER * BLK, BLK), F32)],
        [(OTHER + 1, F32)],
        0.3,
        "backward_own",
    )[0]
    *parts, own, wown = add_core(keep, wkeep, got)
    parts = [shift_y(part, d) for d, part in enumerate(parts, 1)]
    nodes_all = own_rows * lax.axis_size("row") * lax.axis_size("col")
    input_grad, weight_grad = finish(nodes_all ** (-0.5), weight, own, wown, parts)
    return (activated, input_grad, weight_grad)


def solution(mesh):
    placed = (
        P(("col", "row"), None),
        P(),
        P("row", "col", None, None, None),
        P("row", "col", None),
        P("row", "col", None),
        P("row", "col"),
        P(("row", "col"), None),
    )
    return jax.shard_map(
        local,
        mesh=mesh,
        in_specs=placed,
        out_specs=(P(("row", "col"), None), P(("col", "row"), None), P()),
        check_vma=False,
    )
```

```python
import functools

import jax
import jax.numpy as jnp
from jax import lax
from jax.experimental import pallas as pl
from jax.experimental.pallas import tpu as pltpu
from jax.sharding import PartitionSpec as P

BLK = 128
NX = 4
NZ = 4
NY = 4
ROW_BLOCKS = 64
COL_BLOCKS = 32
OWN = 4
F32 = jnp.float32
BF16 = jnp.bfloat16
VMEM_LIMIT = 24 * 1024 * 1024


def vmem_specs(n):
    return [pl.BlockSpec(memory_space=pltpu.VMEM)] * n


def params():
    return pltpu.CompilerParams(vmem_limit_bytes=VMEM_LIMIT)


FAR_F, TWO_F, REST_F, EARLY_B, OTHER_B, OWN_B = range(6)
LISTS = 6
FAR = (NZ - 1) * OWN
OTHER = NY * OWN


def prepare_kernel(packed_ref, adj_ref, blocks_ref, *refs):
    codes_refs, sem = refs[:-1], refs[-1]
    copy = pltpu.make_async_copy(adj_ref, blocks_ref, sem)
    copy.start()
    row, col = lax.axis_index("row"), lax.axis_index("col")
    y, core = row >> 1, row & 1
    x, z = col >> 2, col & 3
    packed = packed_ref[...]
    alive = packed >= 0
    brow, bcol = packed & (ROW_BLOCKS - 1), packed >> 6
    capacity = packed.shape[1]
    slot = lax.broadcasted_iota(jnp.int32, (1, capacity), 1)
    rx, rz, rb = (brow >> 4) & 3, (brow >> 2) & 3, brow & 3
    cy, cc, cb = (bcol >> 3) & 3, (bcol >> 2) & 1, bcol & 3
    ahead, behind, up = (rx - x) & 3, (x - rx) & 3, (cy - y) & 3
    ahead_z, behind_z = (rz - z) & 3, (z - rz) & 3
    other = cc ^ core
    odd, level = ahead & 1, ahead_z == 0
    far = (odd == 1) & (ahead_z > 0)
    rest = (ahead == 0) | ((odd == 1) & level)
    near_row = jnp.where(odd == 1, NZ * OWN + (ahead >> 1) * OWN + rb, ahead_z * OWN + rb)
    to_row = jnp.where(far, (ahead >> 1) * FAR + (ahead_z - 1) * OWN + rb, near_row)
    near_row = jnp.where(odd == 1, NZ * OWN + (behind >> 1) * OWN + rb, behind_z * OWN + rb)
    near_row = jnp.where((ahead == 2) & level, (NZ + 2) * OWN + rb, near_row)
    near_row = jnp.where((ahead == 2) & (ahead_z > 0), near_row - OWN, near_row)
    from_row = jnp.where(far, FAR + (behind >> 1) * FAR + (behind_z - 1) * OWN + rb, near_row)
    to_col = jnp.where((rest | ((ahead == 2) & level)) & (other == 0), OTHER, 0) + up * OWN + cb
    from_col = other * 16 + ((y - cy) & 3) * OWN + cb
    forward_kind = jnp.where(rest, 2, jnp.where(far, 0, 1))
    forward_kind = jnp.where(alive, forward_kind, 3)
    early = rest | ((ahead == 2) & level)
    backward_kind = jnp.where(early, 2, 1 - other)
    backward_kind = jnp.where(alive, backward_kind, 3)
    row_codes = [
        (slot + 512 * to_row + 65536 * from_col).astype(F32),
        (slot + 512 * to_col + 65536 * from_row).astype(F32),
        forward_kind.astype(F32),
        backward_kind.astype(F32),
    ]
    member = [(forward_kind == k).astype(F32) for k in range(3)] + [(backward_kind == k).astype(F32) for k in range(3)]
    counts = [jnp.sum(m, axis=1, keepdims=True) for m in member]
    lists = [jnp.zeros((1, capacity), F32) for _ in range(LISTS)]
    step = 64
    lane = lax.broadcasted_iota(jnp.int32, (step, capacity), 1)
    place = lane.astype(F32)
    for c in range(0, capacity, step):
        sub = lax.broadcasted_iota(jnp.int32, (step, capacity), 0) + c
        fcode, bcode, fkind, bkind = (
            jnp.sum(jnp.where(lane == sub, v, 0.0), axis=1, keepdims=True) for v in row_codes
        )
        ranks = [
            jnp.sum(jnp.where(lane <= sub, m, 0.0), axis=1, keepdims=True) - 1.0 for m in member
        ]
        kinds = [(fkind, 0.0), (fkind, 1.0), (fkind, 2.0), (bkind, 0.0), (bkind, 1.0), (bkind, 2.0)]
        ranks = [jnp.where(kind == k, r, -1.0) for (kind, k), r in zip(kinds, ranks)]
        for q, rank, code in (
            (FAR_F, ranks[0], fcode),
            (TWO_F, ranks[1], fcode),
            (REST_F, ranks[2], fcode),
            (EARLY_B, ranks[5], bcode),
            (OTHER_B, ranks[3], bcode),
            (OWN_B, ranks[4], bcode),
        ):
            lists[q] += jnp.sum(jnp.where(place == rank, code, 0.0), axis=0, keepdims=True)
    where = slot.astype(F32)
    for q, count, idle in (
        (FAR_F, counts[0], 2 * FAR),
        (TWO_F, counts[1], NZ * OWN),
        (REST_F, counts[2], (NZ + 2) * OWN),
        (EARLY_B, counts[5], COL_BLOCKS),
        (OTHER_B, counts[3], OTHER),
        (OWN_B, counts[4], OTHER),
    ):
        codes_refs[q][:, 0:capacity] = jnp.where(where < count, lists[q], 512.0 * idle).astype(jnp.int32)
        codes_refs[q][:, capacity : capacity + BLK] = jnp.broadcast_to(count, (1, BLK)).astype(jnp.int32)
    copy.wait()


def prepare(adjacency, packed):
    capacity = adjacency.shape[0]
    return pl.pallas_call(
        prepare_kernel,
        out_shape=[
            jax.ShapeDtypeStruct(adjacency.shape, adjacency.dtype),
        ]
        + [jax.ShapeDtypeStruct((1, capacity + BLK), jnp.int32)] * LISTS,
        in_specs=vmem_specs(1) + [pl.BlockSpec(memory_space=pl.ANY)],
        out_specs=vmem_specs(1 + LISTS),
        scratch_shapes=[pltpu.SemaphoreType.DMA],
        compiler_params=params(),
        cost_estimate=pl.CostEstimate(flops=0, bytes_accessed=2 * adjacency.size * 2, transcendentals=0),
        name="prepare",
    )(packed, adjacency)


def accumulate(unroll, codes_ref, acc, product):
    @pl.loop(0, pl.cdiv(codes_ref[0, codes_ref.shape[1] - BLK], unroll))
    def _(g):
        codes = [codes_ref[0, g * unroll + j] for j in range(unroll)]
        prods = [product(c & 511, c >> 16) for c in codes]
        for j in range(unroll):
            acc[(codes[j] >> 9) & 127] += prods[j]


def sparse_cost(share):
    return pl.CostEstimate(
        flops=int(512 * BLK**3 * 8 * share), bytes_accessed=int(20 * 2**20 * share), transcendentals=0
    )


def sparse_call(kernel, codes, adjacency, operands, outs, scratch, share, name):
    return pl.pallas_call(
        kernel,
        out_shape=[jax.ShapeDtypeStruct(shape, dtype) for shape, dtype in outs],
        in_specs=[pl.BlockSpec(memory_space=pltpu.SMEM)] + vmem_specs(1 + len(operands)),
        out_specs=vmem_specs(len(outs)),
        scratch_shapes=[pltpu.VMEM((blocks, BLK, BLK), dtype) for blocks, dtype in scratch],
        compiler_params=params(),
        cost_estimate=sparse_cost(share),
        name=name,
    )(codes, adjacency, *operands)


def write_rows(acc, outs):
    at = 0
    for out in outs:
        blocks = out.shape[0] // BLK
        out[...] = acc[pl.ds(at, blocks)].reshape(out.shape).astype(out.dtype)
        at += blocks


def forward_far_kernel(nin, codes_ref, adj_ref, *refs):
    ins, (feats, *outs), acc = refs[:nin], refs[nin:-1], refs[-1]
    per = feats.shape[0] // nin
    for i in range(nin):
        feats[pl.ds(i * per, per)] = ins[i][...].reshape(per, BLK, BLK)
    acc[...] = jnp.zeros_like(acc)

    def product(slot, source):
        return jnp.dot(adj_ref[slot], feats[source], preferred_element_type=F32)

    accumulate(64, codes_ref, acc, product)
    write_rows(acc, outs)


def forward_near_kernel(unroll, codes_ref, adj_ref, feats, *refs):
    outs, acc = refs[:-1], refs[-1]
    acc[...] = jnp.zeros_like(acc)

    def product(slot, source):
        return jnp.dot(adj_ref[slot], feats[source], preferred_element_type=F32)

    accumulate(unroll, codes_ref, acc, product)
    write_rows(acc, outs)


def gather_slopes(slopes, ins):
    at = 0
    for part in ins:
        blocks = part.shape[0] // BLK // OWN * OWN
        slopes[pl.ds(at, blocks)] = part[pl.ds(0, blocks * BLK)].reshape(blocks, BLK, BLK)
        at += blocks


def last_block(part):
    return part[pl.ds(part.shape[0] - BLK, BLK)].astype(F32)


def backward_early_kernel(nin, codes_ref, adj_ref, *refs):
    ins, acc, slopes = refs[:nin], refs[nin], refs[nin + 1]
    gather_slopes(slopes, ins)
    acc[...] = jnp.zeros_like(acc)

    def product(slot, source):
        return jnp.dot(slopes[source], adj_ref[slot], preferred_element_type=F32)

    accumulate(64, codes_ref, acc, product)


def backward_other_kernel(nin, codes_ref, adj_ref, before, rest, level, *refs):
    ins, (send, wsum, slopes), acc = refs[:nin], refs[nin : nin + 3], refs[-1]
    gather_slopes(slopes, ins)
    acc[...] = before[pl.ds(0, OTHER + 1)]

    def product(slot, source):
        return jnp.dot(slopes[source], adj_ref[slot], preferred_element_type=F32)

    accumulate(64, codes_ref, acc, product)
    send[pl.ds(0, OTHER * BLK)] = acc[pl.ds(0, OTHER)].reshape(OTHER * BLK, BLK)
    total = last_block(rest) + last_block(level) + sum(last_block(part) for part in ins)
    wsum[...] = total
    send[pl.ds(OTHER * BLK, BLK)] = total


def backward_own_kernel(codes_ref, adj_ref, before, slopes, keep, acc):
    acc[...] = before[pl.ds(OTHER, OTHER + 1)]

    def product(slot, source):
        return jnp.dot(slopes[source], adj_ref[slot], preferred_element_type=F32)

    accumulate(64, codes_ref, acc, product)
    keep[...] = acc[pl.ds(0, OTHER)].reshape(keep.shape)


def add_split_kernel(nin, *refs):
    ins, outs = refs[:nin], refs[nin:]
    at = 0
    for out in outs:
        rows = out.shape[0]
        total = ins[0][pl.ds(at, rows)].astype(F32)
        for part in ins[1:]:
            total += part[pl.ds(at, rows)].astype(F32)
        out[...] = total.astype(out.dtype)
        at += rows


def add_split(parts, dtypes, name):
    rows = parts[0].shape[0] // len(dtypes)
    return pl.pallas_call(
        functools.partial(add_split_kernel, len(parts)),
        out_shape=[jax.ShapeDtypeStruct((rows, BLK), dtype) for dtype in dtypes],
        in_specs=vmem_specs(len(parts)),
        out_specs=vmem_specs(len(dtypes)),
        compiler_params=params(),
        name=name,
    )(*parts)


def activate_kernel(weight_ref, grad_ref, *refs):
    parts, (act_ref, slope_ref, pay_ref) = refs[:-3], refs[-3:]
    rows = act_ref.shape[0]
    total = parts[0][...]
    for part in parts[1:]:
        total += part[...].astype(F32)
    high = total.astype(BF16)
    rest = total - high.astype(F32)
    low = rest.astype(BF16)
    lowest = (rest - low.astype(F32)).astype(BF16)
    weight = weight_ref[...]
    pre = jnp.dot(lowest, weight, preferred_element_type=F32)
    pre += jnp.dot(low, weight, preferred_element_type=F32)
    pre += jnp.dot(high, weight, preferred_element_type=F32)
    squash = jnp.tanh(pre)
    act_ref[...] = squash.astype(BF16)
    slope = (grad_ref[...].astype(F32) * (1.0 - squash * squash)).astype(BF16)
    wterm = jnp.zeros((BLK, BLK), F32)
    for b in range(0, rows, BLK):
        turned = slope[b : b + BLK].T
        slope_ref[pl.ds(b, BLK)] = turned
        pay_ref[pl.ds(b, BLK)] = turned
        wterm += jnp.dot(turned, high[b : b + BLK], preferred_element_type=F32)
        wterm += jnp.dot(turned, low[b : b + BLK], preferred_element_type=F32)
    pay_ref[pl.ds(rows, BLK)] = wterm.astype(BF16)


def activate(weight, grad_out, parts):
    rows = grad_out.shape[0]
    return pl.pallas_call(
        activate_kernel,
        out_shape=[
            jax.ShapeDtypeStruct((rows, BLK), BF16),
            jax.ShapeDtypeStruct((rows, BLK), BF16),
            jax.ShapeDtypeStruct((rows + BLK, BLK), BF16),
        ],
        in_specs=vmem_specs(2 + len(parts)),
        out_specs=vmem_specs(3),
        compiler_params=params(),
        name="activate",
    )(weight, grad_out, *parts)


def merge_kernel(own, *refs):
    parts, out = refs[:-1], refs[-1]
    rows = own.shape[0] - BLK
    total = last_block(own)
    for i, part in enumerate(parts):
        out[pl.ds(i * rows, rows)] = part[pl.ds(0, rows)]
        total += last_block(part)
    out[pl.ds(len(parts) * rows, BLK)] = total.astype(BF16)


def merge(own, parts):
    rows = len(parts) * (own.shape[0] - BLK) + BLK
    return pl.pallas_call(
        merge_kernel,
        out_shape=jax.ShapeDtypeStruct((rows, BLK), BF16),
        in_specs=vmem_specs(1 + len(parts)),
        out_specs=pl.BlockSpec(memory_space=pltpu.VMEM),
        compiler_params=params(),
        name="merge_z",
    )(own, *parts)


def add_core_kernel(keep, wkeep, got, *outs):
    parts, own, wown = outs[:-2], outs[-2], outs[-1]
    rows = own.shape[0]
    wsum = wkeep[...] + last_block(got)
    wown[...] = wsum
    own[...] = keep[pl.ds(0, rows)] + got[pl.ds(0, rows)]
    for i, part in enumerate(parts, 1):
        part[pl.ds(0, rows)] = (keep[pl.ds(i * rows, rows)] + got[pl.ds(i * rows, rows)]).astype(BF16)
        part[pl.ds(rows, BLK)] = wsum.astype(BF16)


def add_core(keep, wkeep, got):
    rows = keep.shape[0] // NY
    return pl.pallas_call(
        add_core_kernel,
        out_shape=[jax.ShapeDtypeStruct((rows + BLK, BLK), BF16)] * (NY - 1)
        + [jax.ShapeDtypeStruct((rows, BLK), F32), jax.ShapeDtypeStruct((BLK, BLK), F32)],
        in_specs=vmem_specs(3),
        out_specs=vmem_specs(NY + 1),
        compiler_params=params(),
        name="add_core",
    )(keep, wkeep, got)


def finish_kernel(scale, weight_ref, own, wown, *refs):
    parts, (out_ref, wout_ref) = refs[:-2], refs[-2:]
    rows = own.shape[0]
    total, wsum = own[...], wown[...]
    for part in parts:
        total += part[pl.ds(0, rows)].astype(F32)
        wsum += part[pl.ds(rows, BLK)].astype(F32)
    turned = total.astype(BF16)
    for b in range(0, rows, BLK):
        block = jnp.dot(weight_ref[...], turned[b : b + BLK], preferred_element_type=F32)
        out_ref[pl.ds(b, BLK)] = block.T.astype(BF16)
    wout_ref[...] = wsum.T * scale


def finish(scale, weight, own, wown, parts):
    return pl.pallas_call(
        functools.partial(finish_kernel, scale),
        out_shape=[
            jax.ShapeDtypeStruct(own.shape, BF16),
            jax.ShapeDtypeStruct((BLK, BLK), F32),
        ],
        in_specs=vmem_specs(3 + len(parts)),
        out_specs=vmem_specs(2),
        compiler_params=params(),
        name="finish",
    )(weight, own, wown, *parts)


def shift_x(a, d):
    return lax.ppermute(a, "col", [(i, (i // NZ + d) % NX * NZ + i % NZ) for i in range(NX * NZ)])


def shift_z(a, d):
    return lax.ppermute(a, "col", [(i, i // NZ * NZ + (i % NZ + d) % NZ) for i in range(NX * NZ)])


def shift_y(a, d):
    return lax.ppermute(a, "row", [(i, (i // 2 + d) % NY * 2 + i % 2) for i in range(NY * 2)])


def swap_core(a):
    return lax.ppermute(a, "row", [(i, i ^ 1) for i in range(NY * 2)])


def local(features, weight, adjacency, row_index, col_index, block_count, grad_out):
    own_rows = features.shape[0]

    beside = [shift_y(features, d) for d in range(1, NY)]
    alive = jnp.arange(adjacency.shape[2], dtype=jnp.int32)[None] < block_count
    packed = jnp.where(alive, row_index[0] + ROW_BLOCKS * col_index[0], -1)
    blocks, *codes = prepare(adjacency[0, 0], packed)
    beside, blocks, codes = lax.optimization_barrier((beside, blocks, codes))
    mine = [features] + beside
    theirs = [swap_core(a) for a in mine]

    feats, x1, x3 = sparse_call(
        functools.partial(forward_far_kernel, 2 * NY),
        codes[FAR_F],
        blocks,
        mine + theirs,
        [((COL_BLOCKS, BLK, BLK), BF16)] + [((FAR * BLK, BLK), BF16)] * 2,
        [(2 * FAR + 1, F32)],
        0.375,
        "forward_far",
    )
    x1, x3 = shift_x(x1, 1), shift_x(x3, 3)
    across, z1, z2, z3 = sparse_call(
        functools.partial(forward_near_kernel, 32),
        codes[TWO_F],
        blocks,
        [feats],
        [((own_rows, BLK), F32)] + [((own_rows, BLK), BF16)] * 3,
        [(NZ * OWN + 1, F32)],
        0.25,
        "forward_two",
    )
    z1, z2, z3 = shift_z(z1, 1), shift_z(z2, 2), shift_z(z3, 3)
    own, column, n1, n3 = sparse_call(
        functools.partial(forward_near_kernel, 64),
        codes[REST_F],
        blocks,
        [feats],
        [((own_rows, BLK), F32), ((FAR * BLK, BLK), F32)] + [((own_rows, BLK), BF16)] * 2,
        [((NZ + 2) * OWN + 1, F32)],
        0.375,
        "forward_rest",
    )
    from_z = [z1, z2, z3]
    z1, z2, z3 = add_split([column, x1, x3], [BF16] * 3, "add_x")
    across, z1, n1, n3 = lax.optimization_barrier((across, z1, n1, n3))
    z1, z2, z3 = shift_z(z1, 1), shift_z(z2, 2), shift_z(z3, 3)
    across = add_split([across] + from_z, [BF16], "add_z")[0]
    parts = [own, z1, z2, z3, shift_x(n1, 1), shift_x(n3, 3), shift_x(across, 2)]
    activated, slope, pay = activate(weight, grad_out, parts)

    beside = [shift_z(pay, d) for d in range(1, NZ)]
    across = shift_x(pay, 2)
    n1, n3 = shift_x(slope, 1), shift_x(slope, 3)
    rest = merge(pay, beside)
    first, second = shift_x(rest, 1), shift_x(rest, 3)
    across = [across] + [shift_z(across, d) for d in range(1, NZ)]

    part = sparse_call(
        functools.partial(backward_early_kernel, 5),
        codes[EARLY_B],
        blocks,
        [pay, rest, n1, n3, across[0]],
        [((COL_BLOCKS + 1, BLK, BLK), F32)],
        [((NZ + 3) * OWN, BF16)],
        0.375,
        "backward_early",
    )[0]
    late = 3 * FAR
    send, wkeep, slopes = sparse_call(
        functools.partial(backward_other_kernel, NZ + 1),
        codes[OTHER_B],
        blocks,
        [part, rest, across[0]] + across[1:] + [first, second],
        [(((OTHER + 1) * BLK, BLK), F32), ((BLK, BLK), F32), ((late, BLK, BLK), BF16)],
        [(OTHER + 1, F32)],
        0.3,
        "backward_other",
    )
    got = swap_core(send)
    keep = sparse_call(
        backward_own_kernel,
        codes[OWN_B],
        blocks,
        [part, slopes],
        [((OTHER * BLK, BLK), F32)],
        [(OTHER + 1, F32)],
        0.3,
        "backward_own",
    )[0]
    *parts, own, wown = add_core(keep, wkeep, got)
    parts = [shift_y(parts[d - 1], d) for d in (2, 1, 3)]
    nodes_all = own_rows * lax.axis_size("row") * lax.axis_size("col")
    input_grad, weight_grad = finish(nodes_all ** (-0.5), weight, own, wown, parts)
    return (activated, input_grad, weight_grad)


def solution(mesh):
    placed = (
        P(("col", "row"), None),
        P(),
        P("row", "col", None, None, None),
        P("row", "col", None),
        P("row", "col", None),
        P("row", "col"),
        P(("row", "col"), None),
    )
    return jax.shard_map(
        local,
        mesh=mesh,
        in_specs=placed,
        out_specs=(P(("row", "col"), None), P(("col", "row"), None), P()),
        check_vma=False,
    )
```

```python
import functools

import jax
import jax.numpy as jnp
from jax import lax
from jax.experimental import pallas as pl
from jax.experimental.pallas import tpu as pltpu
from jax.sharding import PartitionSpec as P

BLK = 128
NX = 4
NZ = 4
NY = 4
ROW_BLOCKS = 64
COL_BLOCKS = 32
OWN = 4
F32 = jnp.float32
BF16 = jnp.bfloat16
VMEM_LIMIT = 24 * 1024 * 1024


def vmem_specs(n):
    return [pl.BlockSpec(memory_space=pltpu.VMEM)] * n


def params():
    return pltpu.CompilerParams(vmem_limit_bytes=VMEM_LIMIT)


FAR_F, TWO_F, REST_F, EARLY_B, OTHER_B, OWN_B = range(6)
LISTS = 6
FAR = (NZ - 1) * OWN
OTHER = NY * OWN
LOADS = 8


def prepare_kernel(packed_ref, adj_ref, blocks_ref, *refs):
    codes_refs, sems = refs[:-1], refs[-1]
    share = adj_ref.shape[0] // LOADS
    copies = [
        pltpu.make_async_copy(adj_ref.at[pl.ds(i * share, share)], blocks_ref.at[pl.ds(i * share, share)], sems.at[i])
        for i in range(LOADS)
    ]
    live = jnp.sum((packed_ref[...] >= 0).astype(F32)).astype(jnp.int32)
    for i, copy in enumerate(copies):
        pl.when(live > i * share)(copy.start)
    row, col = lax.axis_index("row"), lax.axis_index("col")
    y, core = row >> 1, row & 1
    x, z = col >> 2, col & 3
    packed = packed_ref[...]
    alive = packed >= 0
    brow, bcol = packed & (ROW_BLOCKS - 1), packed >> 6
    capacity = packed.shape[1]
    slot = lax.broadcasted_iota(jnp.int32, (1, capacity), 1)
    rx, rz, rb = (brow >> 4) & 3, (brow >> 2) & 3, brow & 3
    cy, cc, cb = (bcol >> 3) & 3, (bcol >> 2) & 1, bcol & 3
    ahead, behind, up = (rx - x) & 3, (x - rx) & 3, (cy - y) & 3
    ahead_z, behind_z = (rz - z) & 3, (z - rz) & 3
    other = cc ^ core
    odd, level = ahead & 1, ahead_z == 0
    far = (odd == 1) & (ahead_z > 0)
    rest = (ahead == 0) | ((odd == 1) & level)
    near_row = jnp.where(odd == 1, NZ * OWN + (ahead >> 1) * OWN + rb, ahead_z * OWN + rb)
    to_row = jnp.where(far, (ahead >> 1) * FAR + (ahead_z - 1) * OWN + rb, near_row)
    near_row = jnp.where(odd == 1, NZ * OWN + (behind >> 1) * OWN + rb, behind_z * OWN + rb)
    near_row = jnp.where((ahead == 2) & level, (NZ + 2) * OWN + rb, near_row)
    near_row = jnp.where((ahead == 2) & (ahead_z > 0), near_row - OWN, near_row)
    from_row = jnp.where(far, FAR + (behind >> 1) * FAR + (behind_z - 1) * OWN + rb, near_row)
    to_col = jnp.where((rest | ((ahead == 2) & level)) & (other == 0), OTHER, 0) + up * OWN + cb
    from_col = other * 16 + ((y - cy) & 3) * OWN + cb
    forward_kind = jnp.where(rest, 2, jnp.where(far, 0, 1))
    forward_kind = jnp.where(alive, forward_kind, 3)
    early = rest | ((ahead == 2) & level)
    backward_kind = jnp.where(early, 2, 1 - other)
    backward_kind = jnp.where(alive, backward_kind, 3)
    row_codes = [
        (slot + 512 * to_row + 65536 * from_col).astype(F32),
        (slot + 512 * to_col + 65536 * from_row).astype(F32),
        forward_kind.astype(F32),
        backward_kind.astype(F32),
    ]
    member = [(forward_kind == k).astype(F32) for k in range(3)] + [(backward_kind == k).astype(F32) for k in range(3)]
    counts = [jnp.sum(m, axis=1, keepdims=True) for m in member]
    lists = [jnp.zeros((1, capacity), F32) for _ in range(LISTS)]
    step = 64
    lane = lax.broadcasted_iota(jnp.int32, (step, capacity), 1)
    place = lane.astype(F32)
    for c in range(0, capacity, step):
        sub = lax.broadcasted_iota(jnp.int32, (step, capacity), 0) + c
        fcode, bcode, fkind, bkind = (
            jnp.sum(jnp.where(lane == sub, v, 0.0), axis=1, keepdims=True) for v in row_codes
        )
        ranks = [
            jnp.sum(jnp.where(lane <= sub, m, 0.0), axis=1, keepdims=True) - 1.0 for m in member
        ]
        kinds = [(fkind, 0.0), (fkind, 1.0), (fkind, 2.0), (bkind, 0.0), (bkind, 1.0), (bkind, 2.0)]
        ranks = [jnp.where(kind == k, r, -1.0) for (kind, k), r in zip(kinds, ranks)]
        for q, rank, code in (
            (FAR_F, ranks[0], fcode),
            (TWO_F, ranks[1], fcode),
            (REST_F, ranks[2], fcode),
            (EARLY_B, ranks[5], bcode),
            (OTHER_B, ranks[3], bcode),
            (OWN_B, ranks[4], bcode),
        ):
            lists[q] += jnp.sum(jnp.where(place == rank, code, 0.0), axis=0, keepdims=True)
    where = slot.astype(F32)
    for q, count, idle in (
        (FAR_F, counts[0], 2 * FAR),
        (TWO_F, counts[1], NZ * OWN),
        (REST_F, counts[2], (NZ + 2) * OWN),
        (EARLY_B, counts[5], COL_BLOCKS),
        (OTHER_B, counts[3], OTHER),
        (OWN_B, counts[4], OTHER),
    ):
        codes_refs[q][:, 0:capacity] = jnp.where(where < count, lists[q], 512.0 * idle).astype(jnp.int32)
        codes_refs[q][:, capacity : capacity + BLK] = jnp.broadcast_to(count, (1, BLK)).astype(jnp.int32)
    for i, copy in enumerate(copies):
        pl.when(live > i * share)(copy.wait)


def prepare(adjacency, packed):
    capacity = adjacency.shape[0]
    return pl.pallas_call(
        prepare_kernel,
        out_shape=[
            jax.ShapeDtypeStruct(adjacency.shape, adjacency.dtype),
        ]
        + [jax.ShapeDtypeStruct((1, capacity + BLK), jnp.int32)] * LISTS,
        in_specs=vmem_specs(1) + [pl.BlockSpec(memory_space=pl.ANY)],
        out_specs=vmem_specs(1 + LISTS),
        scratch_shapes=[pltpu.SemaphoreType.DMA((LOADS,))],
        compiler_params=params(),
        cost_estimate=pl.CostEstimate(flops=0, bytes_accessed=2 * adjacency.size * 2, transcendentals=0),
        name="prepare",
    )(packed, adjacency)


def accumulate(unroll, codes_ref, acc, product):
    @pl.loop(0, pl.cdiv(codes_ref[0, codes_ref.shape[1] - BLK], unroll))
    def _(g):
        codes = [codes_ref[0, g * unroll + j] for j in range(unroll)]
        prods = [product(c & 511, c >> 16) for c in codes]
        for j in range(unroll):
            acc[(codes[j] >> 9) & 127] += prods[j]


def sparse_cost(share):
    return pl.CostEstimate(
        flops=int(512 * BLK**3 * 8 * share), bytes_accessed=int(20 * 2**20 * share), transcendentals=0
    )


def sparse_call(kernel, codes, adjacency, operands, outs, scratch, share, name):
    return pl.pallas_call(
        kernel,
        out_shape=[jax.ShapeDtypeStruct(shape, dtype) for shape, dtype in outs],
        in_specs=[pl.BlockSpec(memory_space=pltpu.SMEM)] + vmem_specs(1 + len(operands)),
        out_specs=vmem_specs(len(outs)),
        scratch_shapes=[pltpu.VMEM((blocks, BLK, BLK), dtype) for blocks, dtype in scratch],
        compiler_params=params(),
        cost_estimate=sparse_cost(share),
        name=name,
    )(codes, adjacency, *operands)


def write_rows(acc, outs):
    at = 0
    for out in outs:
        blocks = out.shape[0] // BLK
        out[...] = acc[pl.ds(at, blocks)].reshape(out.shape).astype(out.dtype)
        at += blocks


def forward_far_kernel(nin, codes_ref, adj_ref, *refs):
    ins, (feats, *outs), acc = refs[:nin], refs[nin:-1], refs[-1]
    per = feats.shape[0] // nin
    for i in range(nin):
        feats[pl.ds(i * per, per)] = ins[i][...].reshape(per, BLK, BLK)
    acc[...] = jnp.zeros_like(acc)

    def product(slot, source):
        return jnp.dot(adj_ref[slot], feats[source], preferred_element_type=F32)

    accumulate(64, codes_ref, acc, product)
    write_rows(acc, outs)


def forward_near_kernel(unroll, codes_ref, adj_ref, feats, *refs):
    outs, acc = refs[:-1], refs[-1]
    acc[...] = jnp.zeros_like(acc)

    def product(slot, source):
        return jnp.dot(adj_ref[slot], feats[source], preferred_element_type=F32)

    accumulate(unroll, codes_ref, acc, product)
    write_rows(acc, outs)


def gather_slopes(slopes, ins):
    at = 0
    for part in ins:
        blocks = part.shape[0] // BLK - 1
        slopes[pl.ds(at, blocks)] = part[pl.ds(0, blocks * BLK)].reshape(blocks, BLK, BLK)
        at += blocks


def last_block(part):
    return part[pl.ds(part.shape[0] - BLK, BLK)].astype(F32)


def backward_early_kernel(nin, codes_ref, adj_ref, *refs):
    ins, acc, slopes = refs[:nin], refs[nin], refs[nin + 1]
    gather_slopes(slopes, ins)
    acc[...] = jnp.zeros_like(acc)

    def product(slot, source):
        return jnp.dot(slopes[source], adj_ref[slot], preferred_element_type=F32)

    accumulate(64, codes_ref, acc, product)


def backward_other_kernel(nin, codes_ref, adj_ref, before, rest, level, *refs):
    ins, (send, wsum, slopes), acc = refs[:nin], refs[nin : nin + 3], refs[-1]
    gather_slopes(slopes, ins)
    acc[...] = before[pl.ds(0, OTHER + 1)]

    def product(slot, source):
        return jnp.dot(slopes[source], adj_ref[slot], preferred_element_type=F32)

    accumulate(64, codes_ref, acc, product)
    send[pl.ds(0, OTHER * BLK)] = acc[pl.ds(0, OTHER)].reshape(OTHER * BLK, BLK)
    total = last_block(rest) + last_block(level) + sum(last_block(part) for part in ins)
    wsum[...] = total
    send[pl.ds(OTHER * BLK, BLK)] = total


def backward_own_kernel(codes_ref, adj_ref, before, slopes, keep, acc):
    acc[...] = before[pl.ds(OTHER, OTHER + 1)]

    def product(slot, source):
        return jnp.dot(slopes[source], adj_ref[slot], preferred_element_type=F32)

    accumulate(64, codes_ref, acc, product)
    keep[...] = acc[pl.ds(0, OTHER)].reshape(keep.shape)


def add_split_kernel(nin, *refs):
    ins, outs = refs[:nin], refs[nin:]
    at = 0
    for out in outs:
        rows = out.shape[0]
        total = ins[0][pl.ds(at, rows)].astype(F32)
        for part in ins[1:]:
            total += part[pl.ds(at, rows)].astype(F32)
        out[...] = total.astype(out.dtype)
        at += rows


def add_split(parts, dtypes, name):
    rows = parts[0].shape[0] // len(dtypes)
    return pl.pallas_call(
        functools.partial(add_split_kernel, len(parts)),
        out_shape=[jax.ShapeDtypeStruct((rows, BLK), dtype) for dtype in dtypes],
        in_specs=vmem_specs(len(parts)),
        out_specs=vmem_specs(len(dtypes)),
        compiler_params=params(),
        name=name,
    )(*parts)


def activate_kernel(weight_ref, grad_ref, *refs):
    parts, (act_ref, pay_ref) = refs[:-2], refs[-2:]
    rows = act_ref.shape[0]
    total = parts[0][...]
    for part in parts[1:]:
        total += part[...].astype(F32)
    high = total.astype(BF16)
    rest = total - high.astype(F32)
    low = rest.astype(BF16)
    lowest = (rest - low.astype(F32)).astype(BF16)
    weight = weight_ref[...]
    pre = jnp.dot(lowest, weight, preferred_element_type=F32)
    pre += jnp.dot(low, weight, preferred_element_type=F32)
    pre += jnp.dot(high, weight, preferred_element_type=F32)
    squash = jnp.tanh(pre)
    act_ref[...] = squash.astype(BF16)
    slope = (grad_ref[...].astype(F32) * (1.0 - squash * squash)).astype(BF16)
    wterm = jnp.zeros((BLK, BLK), F32)
    for b in range(0, rows, BLK):
        turned = slope[b : b + BLK].T
        pay_ref[pl.ds(b, BLK)] = turned
        wterm += jnp.dot(turned, high[b : b + BLK], preferred_element_type=F32)
        wterm += jnp.dot(turned, low[b : b + BLK], preferred_element_type=F32)
    pay_ref[pl.ds(rows, BLK)] = wterm.astype(BF16)


def activate(weight, grad_out, parts):
    rows = grad_out.shape[0]
    return pl.pallas_call(
        activate_kernel,
        out_shape=[
            jax.ShapeDtypeStruct((rows, BLK), BF16),
            jax.ShapeDtypeStruct((rows + BLK, BLK), BF16),
        ],
        in_specs=vmem_specs(2 + len(parts)),
        out_specs=vmem_specs(2),
        compiler_params=params(),
        name="activate",
    )(weight, grad_out, *parts)


def merge_kernel(own, *refs):
    parts, out = refs[:-1], refs[-1]
    rows = own.shape[0] - BLK
    total = last_block(own)
    for i, part in enumerate(parts):
        out[pl.ds(i * rows, rows)] = part[pl.ds(0, rows)]
        total += last_block(part)
    out[pl.ds(len(parts) * rows, BLK)] = total.astype(BF16)


def merge(own, parts):
    rows = len(parts) * (own.shape[0] - BLK) + BLK
    return pl.pallas_call(
        merge_kernel,
        out_shape=jax.ShapeDtypeStruct((rows, BLK), BF16),
        in_specs=vmem_specs(1 + len(parts)),
        out_specs=pl.BlockSpec(memory_space=pltpu.VMEM),
        compiler_params=params(),
        name="merge_z",
    )(own, *parts)


def add_core_kernel(keep, wkeep, got, *outs):
    parts, own, wown = outs[:-2], outs[-2], outs[-1]
    rows = own.shape[0]
    wsum = wkeep[...] + last_block(got)
    wown[...] = wsum
    own[...] = keep[pl.ds(0, rows)] + got[pl.ds(0, rows)]
    for i, part in enumerate(parts, 1):
        part[pl.ds(0, rows)] = (keep[pl.ds(i * rows, rows)] + got[pl.ds(i * rows, rows)]).astype(BF16)
        part[pl.ds(rows, BLK)] = wsum.astype(BF16)


def add_core(keep, wkeep, got):
    rows = keep.shape[0] // NY
    return pl.pallas_call(
        add_core_kernel,
        out_shape=[jax.ShapeDtypeStruct((rows + BLK, BLK), BF16)] * (NY - 1)
        + [jax.ShapeDtypeStruct((rows, BLK), F32), jax.ShapeDtypeStruct((BLK, BLK), F32)],
        in_specs=vmem_specs(3),
        out_specs=vmem_specs(NY + 1),
        compiler_params=params(),
        name="add_core",
    )(keep, wkeep, got)


def finish_kernel(scale, weight_ref, own, wown, *refs):
    parts, (out_ref, wout_ref) = refs[:-2], refs[-2:]
    rows = own.shape[0]
    total, wsum = own[...], wown[...]
    for part in parts:
        total += part[pl.ds(0, rows)].astype(F32)
        wsum += part[pl.ds(rows, BLK)].astype(F32)
    turned = total.astype(BF16)
    for b in range(0, rows, BLK):
        block = jnp.dot(weight_ref[...], turned[b : b + BLK], preferred_element_type=F32)
        out_ref[pl.ds(b, BLK)] = block.T.astype(BF16)
    wout_ref[...] = wsum.T * scale


def finish(scale, weight, own, wown, parts):
    return pl.pallas_call(
        functools.partial(finish_kernel, scale),
        out_shape=[
            jax.ShapeDtypeStruct(own.shape, BF16),
            jax.ShapeDtypeStruct((BLK, BLK), F32),
        ],
        in_specs=vmem_specs(3 + len(parts)),
        out_specs=vmem_specs(2),
        compiler_params=params(),
        name="finish",
    )(weight, own, wown, *parts)


def shift_x(a, d):
    return lax.ppermute(a, "col", [(i, (i // NZ + d) % NX * NZ + i % NZ) for i in range(NX * NZ)])


def shift_z(a, d):
    return lax.ppermute(a, "col", [(i, i // NZ * NZ + (i % NZ + d) % NZ) for i in range(NX * NZ)])


def shift_y(a, d):
    return lax.ppermute(a, "row", [(i, (i // 2 + d) % NY * 2 + i % 2) for i in range(NY * 2)])


def swap_core(a):
    return lax.ppermute(a, "row", [(i, i ^ 1) for i in range(NY * 2)])


def local(features, weight, adjacency, row_index, col_index, block_count, grad_out):
    own_rows = features.shape[0]

    beside = [shift_y(features, d) for d in range(1, NY)]
    alive = jnp.arange(adjacency.shape[2], dtype=jnp.int32)[None] < block_count
    packed = jnp.where(alive, row_index[0] + ROW_BLOCKS * col_index[0], -1)
    blocks, *codes = prepare(adjacency[0, 0], packed)
    beside, blocks, codes = lax.optimization_barrier((beside, blocks, codes))
    mine = [features] + beside
    theirs = [swap_core(a) for a in mine]

    feats, x1, x3 = sparse_call(
        functools.partial(forward_far_kernel, 2 * NY),
        codes[FAR_F],
        blocks,
        mine + theirs,
        [((COL_BLOCKS, BLK, BLK), BF16)] + [((FAR * BLK, BLK), BF16)] * 2,
        [(2 * FAR + 1, F32)],
        0.375,
        "forward_far",
    )
    x1, x3 = shift_x(x1, 1), shift_x(x3, 3)
    across, z1, z2, z3 = sparse_call(
        functools.partial(forward_near_kernel, 32),
        codes[TWO_F],
        blocks,
        [feats],
        [((own_rows, BLK), F32)] + [((own_rows, BLK), BF16)] * 3,
        [(NZ * OWN + 1, F32)],
        0.25,
        "forward_two",
    )
    z1, z2, z3 = shift_z(z1, 1), shift_z(z2, 2), shift_z(z3, 3)
    own, column, n1, n3 = sparse_call(
        functools.partial(forward_near_kernel, 64),
        codes[REST_F],
        blocks,
        [feats],
        [((own_rows, BLK), F32), ((FAR * BLK, BLK), F32)] + [((own_rows, BLK), BF16)] * 2,
        [((NZ + 2) * OWN + 1, F32)],
        0.375,
        "forward_rest",
    )
    from_z = [z1, z2, z3]
    z1, z2, z3 = add_split([column, x1, x3], [BF16] * 3, "add_x")
    across, z1, n1, n3 = lax.optimization_barrier((across, z1, n1, n3))
    z1, z2, z3 = shift_z(z1, 1), shift_z(z2, 2), shift_z(z3, 3)
    across = add_split([across] + from_z, [BF16], "add_z")[0]
    parts = [own, z1, z2, z3, shift_x(n1, 1), shift_x(n3, 3), shift_x(across, 2)]
    activated, pay = activate(weight, grad_out, parts)

    beside = [shift_z(pay, d) for d in range(1, NZ)]
    across = shift_x(pay, 2)
    n1, n3 = shift_x(pay, 1), shift_x(pay, 3)
    rest = merge(pay, beside)
    first, second = shift_x(rest, 1), shift_x(rest, 3)
    across = [across] + [shift_z(across, d) for d in range(1, NZ)]

    part = sparse_call(
        functools.partial(backward_early_kernel, 5),
        codes[EARLY_B],
        blocks,
        [pay, rest, n1, n3, across[0]],
        [((COL_BLOCKS + 1, BLK, BLK), F32)],
        [((NZ + 3) * OWN, BF16)],
        0.375,
        "backward_early",
    )[0]
    late = 3 * FAR
    send, wkeep, slopes = sparse_call(
        functools.partial(backward_other_kernel, NZ + 1),
        codes[OTHER_B],
        blocks,
        [part, rest, across[0]] + across[1:] + [first, second],
        [(((OTHER + 1) * BLK, BLK), F32), ((BLK, BLK), F32), ((late, BLK, BLK), BF16)],
        [(OTHER + 1, F32)],
        0.3,
        "backward_other",
    )
    got = swap_core(send)
    keep = sparse_call(
        backward_own_kernel,
        codes[OWN_B],
        blocks,
        [part, slopes],
        [((OTHER * BLK, BLK), F32)],
        [(OTHER + 1, F32)],
        0.3,
        "backward_own",
    )[0]
    *parts, own, wown = add_core(keep, wkeep, got)
    parts = [shift_y(part, d) for d, part in enumerate(parts, 1)]
    nodes_all = own_rows * lax.axis_size("row") * lax.axis_size("col")
    input_grad, weight_grad = finish(nodes_all ** (-0.5), weight, own, wown, parts)
    return (activated, input_grad, weight_grad)


def solution(mesh):
    placed = (
        P(("col", "row"), None),
        P(),
        P("row", "col", None, None, None),
        P("row", "col", None),
        P("row", "col", None),
        P("row", "col"),
        P(("row", "col"), None),
    )
    return jax.shard_map(
        local,
        mesh=mesh,
        in_specs=placed,
        out_specs=(P(("row", "col"), None), P(("col", "row"), None), P()),
        check_vma=False,
    )
```
